32 devices in a mesh: row: 4 (over z), col: 2 (over y), seq: 4 (over x, core).
Axes of the slice: x: 2, y: 2, z: 4, core: 2. Of those that a mesh axis runs over, the one named last changes fastest.
Arguments:
- latent: bfloat16 [24, 64, 64, 4], P('seq', 'row', 'col'), may hold values from -6 to 6
- conditioning: bfloat16 [24, 4, 1152], P('seq'), may hold values from -6 to 6
- segment_ids: int32 [24, 32, 32], P('seq'), may hold values from 0 to 3, as said below
- positions: int32 [24, 32, 32, 2], P('seq', 'row', 'col'), may hold values from 0 to 31, as said below
- cotangent: bfloat16 [24, 64, 64, 8], P('seq', 'row', 'col'), may hold values from -6 to 6
- w_embed: bfloat16 [16, 1152], replicated, may hold values from -1.5 to 1.5
- b_embed: bfloat16 [1152], P(('row', 'col', 'seq')), may hold values from -1.1953125 to 1.1953125
- w_mod: bfloat16 [1152, 6912], P(('row', 'col', 'seq')), may hold values from -0.1875 to 0.1875
- b_mod: bfloat16 [6912], P(('row', 'col', 'seq')), may hold values from -1.796875 to 1.796875
- w_qkv: bfloat16 [1152, 3456], P(('row', 'col', 'seq')), may hold values from -0.1875 to 0.1875
- b_query: bfloat16 [1152], P(('row', 'col', 'seq')), may hold values from -1.1953125 to 1.1953125
- b_value: bfloat16 [1152], P(('row', 'col', 'seq')), may hold values from -1.1953125 to 1.1953125
- w_proj: bfloat16 [1152, 1152], P(('row', 'col', 'seq')), may hold values from -1.5 to 1.5
- b_proj: bfloat16 [1152], P(('row', 'col', 'seq')), may hold values from -1.1953125 to 1.1953125
- w_up: bfloat16 [1152, 4608], P(('row', 'col', 'seq')), may hold values from -0.1875 to 0.1875
- b_up: bfloat16 [4608], P(('row', 'col', 'seq')), may hold values from -1.1953125 to 1.1953125
- w_down: bfloat16 [4608, 1152], P(('row', 'col', 'seq')), may hold values from -0.09375 to 0.09375
- b_down: bfloat16 [1152], P(('row', 'col', 'seq')), may hold values from -1.1953125 to 1.1953125
- w_final_mod: bfloat16 [1152, 2304], P(('row', 'col', 'seq')), may hold values from -0.1875 to 0.1875
- b_final_mod: bfloat16 [2304], P(('row', 'col', 'seq')), may hold values from -1.796875 to 1.796875
- w_out: bfloat16 [1152, 32], P(('row', 'col', 'seq')), may hold values from -0.1875 to 0.1875
- b_out: bfloat16 [32], replicated, may hold values from -1.1953125 to 1.1953125
Outputs:
- prediction: bfloat16 [24, 64, 64, 8], P('seq', 'row', 'col')
- grad_latent: float32 [24, 64, 64, 4], P('seq', 'row', 'col')
- grad_conditioning: float32 [24, 4, 1152], P('seq')
- grad_w_embed: float32 [16, 1152], replicated
- grad_b_embed: float32 [1152], P(('row', 'col', 'seq'))
- grad_w_mod: float32 [1152, 6912], P(('row', 'col', 'seq'))
- grad_b_mod: float32 [6912], P(('row', 'col', 'seq'))
- grad_w_qkv: float32 [1152, 3456], P(('row', 'col', 'seq'))
- grad_b_query: float32 [1152], P(('row', 'col', 'seq'))
- grad_b_value: float32 [1152], P(('row', 'col', 'seq'))
- grad_w_proj: float32 [1152, 1152], P(('row', 'col', 'seq'))
- grad_b_proj: float32 [1152], P(('row', 'col', 'seq'))
- grad_w_up: float32 [1152, 4608], P(('row', 'col', 'seq'))
- grad_b_up: float32 [4608], P(('row', 'col', 'seq'))
- grad_w_down: float32 [4608, 1152], P(('row', 'col', 'seq'))
- grad_b_down: float32 [1152], P(('row', 'col', 'seq'))
- grad_w_final_mod: float32 [1152, 2304], P(('row', 'col', 'seq'))
- grad_b_final_mod: float32 [2304], P(('row', 'col', 'seq'))
- grad_w_out: float32 [1152, 32], P(('row', 'col', 'seq'))
- grad_b_out: float32 [32], replicated
The draws below stay inside these ranges and needn't reach their ends.
Inputs may be any that keep to these rules, and one draw needn't show every extreme that they name: `segment_ids`: each sequence's grid is cut into rectangular crops: a row cut, and a column cut in the upper and in the lower band, giving crops 0 (upper left), 1 (upper right), 2 (lower left), 3 (lower right); in each aligned group of 6 sequences one sequence is a single crop 0 covering the whole grid. `positions`: row and column of each patch counted from the top left corner of its crop (as given by segment_ids).
All inputs are finite; a program needn't handle non-finite values.
Results may differ from the reference program's by a relative error of at most 0.014.
Values may be sent and summed in bfloat16 or wider, within the bound.
No kernel may reach another device: no remote copies, remote signals or barrier semaphores. Data moves between devices by JAX's collectives and lax.ppermute only.
A program may use at most 384 MiB of HBM per device.

```python
import math
import jax
import jax.numpy as jnp
from jax import lax

D = 1152
HEADS = 16
HDIM = 72
FF = 4608
CIN = 4
COUT = 8
PATCH = 2
GRID = 32
SEGS = 4
SEQ_DEV = 6
SEQS = 24
P_IN = 16
P_OUT = 32


def crop_layout(key):
    groups = SEQS // SEQ_DEV
    cut_key, pick_key = jax.random.split(key)
    cut_values = jax.random.randint(cut_key, (SEQS, 3), 1, GRID)
    single_pick = jax.random.randint(pick_key, (groups,), 0, SEQ_DEV)
    single_seq = jnp.arange(SEQS) % SEQ_DEV == jnp.repeat(single_pick, SEQ_DEV)
    row_index = jnp.arange(GRID, dtype=jnp.int32)[None, :, None]
    col_index = jnp.arange(GRID, dtype=jnp.int32)[None, None, :]
    cut_row = cut_values[:, 0][:, None, None]
    cut_col = jnp.where(row_index < cut_row, cut_values[:, 1][:, None, None], cut_values[:, 2][:, None, None])
    lower_part = row_index >= cut_row
    right_part = col_index >= cut_col
    crops = lower_part.astype(jnp.int32) * 2 + right_part.astype(jnp.int32)
    pos_row = row_index - jnp.where(lower_part, cut_row, 0)
    pos_col = col_index - jnp.where(right_part, cut_col, 0)
    single_mask = single_seq[:, None, None]
    crops = jnp.where(single_mask, 0, crops)
    pos_row = jnp.where(single_mask, row_index, pos_row)
    pos_col = jnp.where(single_mask, col_index, pos_col)
    pos_row = jnp.broadcast_to(pos_row, (SEQS, GRID, GRID))
    pos_col = jnp.broadcast_to(pos_col, (SEQS, GRID, GRID))
    return (crops.astype(jnp.int32), jnp.stack([pos_row, pos_col], axis=-1).astype(jnp.int32))


def draw_segment_ids(key, part):
    layout = crop_layout(key)
    return layout[0]


def draw_positions(key, part):
    layout = crop_layout(key)
    return layout[1]


def level_of(stream_key, extent, pieces, smallest, largest):
    level, own = 1.0, jax.random.fold_in(stream_key, 6)
    for position, blocks in pieces:
        heights = jnp.exp(jax.random.uniform(jax.random.fold_in(own, position), (blocks,), jnp.float32, smallest / len(pieces), largest / len(pieces)))
        level = level * jnp.repeat(heights, extent[position] // blocks).reshape([-1 if axis == position else 1 for axis in range(len(extent))])
    return level


def bell_draw(key, dims, scale, most, shards=(), kind=jnp.bfloat16):
    values = jax.random.normal(key, dims, jnp.float32) * scale
    if len(shards) > 0:
        values = level_of(key, dims, shards, -0.22, 0.18) * values
    return jnp.clip(values, min=-most, max=most).astype(kind)


def setup_inputs(seed: int = 0) -> dict:
    keys = jax.random.split(jax.random.key(seed), 23)
    latent = bell_draw(keys[0], (SEQS, PATCH * GRID, PATCH * GRID, CIN), 1.0, 6.0, ((0, 4), (1, 4), (2, 2)))
    conditioning = bell_draw(keys[1], (SEQS, SEGS, D), 1.0, 6.0, ((0, 4),))
    segment_ids = draw_segment_ids(jax.random.fold_in(keys[22], 71), 0)
    positions = draw_positions(jax.random.fold_in(keys[22], 71), 0)
    cotangent = bell_draw(keys[4], (SEQS, PATCH * GRID, PATCH * GRID, COUT), 1.0, 6.0, ((0, 4), (1, 4), (2, 2)))
    w_embed = bell_draw(keys[5], (P_IN, D), P_IN ** -0.5, 1.5)
    b_embed = bell_draw(keys[6], (D,), 0.2, 1.1953125, ((0, 32),))
    w_mod = bell_draw(keys[7], (D, 6 * D), D ** -0.5, 0.1875, ((0, 32),))
    b_mod = bell_draw(keys[8], (6 * D,), 0.3, 1.796875, ((0, 32),))
    w_qkv = bell_draw(keys[9], (D, 3 * D), D ** -0.5, 0.1875, ((0, 32),))
    b_query = bell_draw(keys[10], (D,), 0.2, 1.1953125, ((0, 32),))
    b_value = bell_draw(keys[11], (D,), 0.2, 1.1953125, ((0, 32),))
    w_proj = bell_draw(keys[12], (D, D), (D // 64) ** -0.5, 1.5, ((0, 32),))
    b_proj = bell_draw(keys[13], (D,), 0.2, 1.1953125, ((0, 32),))
    w_up = bell_draw(keys[14], (D, FF), D ** -0.5, 0.1875, ((0, 32),))
    b_up = bell_draw(keys[15], (FF,), 0.2, 1.1953125, ((0, 32),))
    w_down = bell_draw(keys[16], (FF, D), FF ** -0.5, 0.09375, ((0, 32),))
    b_down = bell_draw(keys[17], (D,), 0.2, 1.1953125, ((0, 32),))
    w_final_mod = bell_draw(keys[18], (D, 2 * D), D ** -0.5, 0.1875, ((0, 32),))
    b_final_mod = bell_draw(keys[19], (2 * D,), 0.3, 1.796875, ((0, 32),))
    w_out = bell_draw(keys[20], (D, P_OUT), D ** -0.5, 0.1875, ((0, 32),))
    b_out = bell_draw(keys[21], (P_OUT,), 0.2, 1.1953125)
    return dict(latent=latent, conditioning=conditioning, segment_ids=segment_ids, positions=positions, cotangent=cotangent, w_embed=w_embed, b_embed=b_embed, w_mod=w_mod, b_mod=b_mod, w_qkv=w_qkv, b_query=b_query, b_value=b_value, w_proj=w_proj, b_proj=b_proj, w_up=w_up, b_up=b_up, w_down=w_down, b_down=b_down, w_final_mod=w_final_mod, b_final_mod=b_final_mod, w_out=w_out, b_out=b_out)


@jax.custom_vjp
def low(v):
    return lax.optimization_barrier(v.astype(jnp.bfloat16)).astype(jnp.float32)

@jax.custom_vjp
def low_back(v):
    return v

def low_keep(v):
    return (low(v), None)

def low_pass(kept, grad):
    return (grad,)

def back_keep(v):
    return (v, None)

def back_low(kept, grad):
    return (low(grad),)
low.defvjp(low_keep, low_pass)
low_back.defvjp(back_keep, back_low)
HIGHEST = lax.Precision.HIGHEST

def product(left, right):
    return jnp.einsum('...i,ij->...j', left, right, precision=HIGHEST)

def modulated_norm(stream, shift_vec, scale_vec):
    average = lax.optimization_barrier(jnp.mean(stream, axis=-1, keepdims=True))
    centred = stream - average
    spread = lax.optimization_barrier(jnp.mean(centred * centred, axis=-1, keepdims=True))
    return centred * lax.rsqrt(spread + 1e-06) * (1.0 + scale_vec) + shift_vec

def position_table(positions, model_width):
    quarter = model_width // 4
    powers = jnp.arange(quarter, dtype=jnp.float32) / quarter
    frequency = jnp.exp(powers * -math.log(10000.0))
    row_angle = positions[..., 0:1].astype(jnp.float32) * frequency
    col_angle = positions[..., 1:2].astype(jnp.float32) * frequency
    return jnp.concatenate([jnp.sin(row_angle), jnp.cos(row_angle), jnp.sin(col_angle), jnp.cos(col_angle)], axis=-1)

def attention_one(operands):
    queries, key_rows, value_rows, seg_ids = operands
    logits = jnp.einsum('qhd,khd->hqk', queries, key_rows, precision=HIGHEST) * (1.0 / math.sqrt(HDIM))
    same_crop = seg_ids[:, None] == seg_ids[None, :]
    logits = low_back(jnp.where(same_crop[None], logits, -1e+30))
    highest = lax.optimization_barrier(jnp.max(logits, axis=-1, keepdims=True))
    weights_raw = jnp.exp(logits - highest)
    probability = weights_raw / lax.optimization_barrier(jnp.sum(weights_raw, axis=-1, keepdims=True))
    return jnp.einsum('hqk,khd->qhd', low(probability), value_rows, precision=HIGHEST)

def group_forward(params, latent_part, cond_part, segments, position_part):
    w_embed, b_embed, w_mod, b_mod, w_qkv, b_query, b_value, w_proj, b_proj, w_up, b_up, w_down, b_down, w_final_mod, b_final_mod, w_out, b_out = params
    count = latent_part.shape[0]
    tokens_all = GRID * GRID
    patches = latent_part.reshape(count, GRID, PATCH, GRID, PATCH, CIN).transpose(0, 1, 3, 2, 4, 5)
    patches = patches.reshape(count, tokens_all, PATCH * PATCH * CIN)
    embedded = product(patches, w_embed) + b_embed + position_table(position_part.reshape(count, tokens_all, 2), D)
    cond_low = low(jax.nn.silu(cond_part))
    modulation = low_back(product(cond_low, w_mod) + b_mod)
    final_modulation = low_back(product(cond_low, w_final_mod) + b_final_mod)
    seg_flat = segments.reshape(count, tokens_all)
    crop_onehot = (seg_flat[:, :, None] == jnp.arange(SEGS, dtype=jnp.int32)).astype(jnp.float32)
    mod_tokens = jnp.einsum('stg,sge->ste', crop_onehot, modulation, precision=HIGHEST)
    final_tokens = jnp.einsum('stg,sge->ste', crop_onehot, final_modulation, precision=HIGHEST)
    shift_one, scale_one, gate_one, shift_two, scale_two, gate_two = jnp.split(mod_tokens, 6, axis=-1)
    shift_three, scale_three = jnp.split(final_tokens, 2, axis=-1)
    hidden_one = low(modulated_norm(embedded, shift_one, scale_one))
    qkv_bias = jnp.concatenate([b_query, jnp.zeros_like(b_query), b_value])
    qkv = low(low_back(product(hidden_one, w_qkv) + qkv_bias))
    queries, key_rows, value_rows = jnp.split(qkv, 3, axis=-1)
    queries = queries.reshape(count, tokens_all, HEADS, HDIM)
    key_rows = key_rows.reshape(count, tokens_all, HEADS, HDIM)
    value_rows = value_rows.reshape(count, tokens_all, HEADS, HDIM)
    attended = lax.map(jax.checkpoint(attention_one), (queries, key_rows, value_rows, seg_flat))
    attended = low(low_back(attended.reshape(count, tokens_all, D)))
    projected = low_back(product(attended, w_proj) + b_proj)
    mixed_one = embedded + gate_one * projected
    hidden_two = low(modulated_norm(mixed_one, shift_two, scale_two))
    pre_act = low_back(product(hidden_two, w_up) + b_up)
    activated = low(jax.nn.gelu(pre_act, approximate=True))
    mlp_out = low_back(product(activated, w_down) + b_down)
    mixed_two = mixed_one + gate_two * mlp_out
    hidden_three = low(modulated_norm(mixed_two, shift_three, scale_three))
    token_out = product(hidden_three, w_out) + b_out
    laid = token_out.reshape(count, GRID, GRID, PATCH, PATCH, COUT).transpose(0, 1, 3, 2, 4, 5)
    return laid.reshape(count, GRID * PATCH, GRID * PATCH, COUT)

def reference(latent, conditioning, segment_ids, positions, cotangent, w_embed, b_embed, w_mod, b_mod, w_qkv, b_query, b_value, w_proj, b_proj, w_up, b_up, w_down, b_down, w_final_mod, b_final_mod, w_out, b_out):
    params = tuple((weight.astype(jnp.float32) for weight in (w_embed, b_embed, w_mod, b_mod, w_qkv, b_query, b_value, w_proj, b_proj, w_up, b_up, w_down, b_down, w_final_mod, b_final_mod, w_out, b_out)))
    group_size = math.gcd(SEQS, 4)
    groups = SEQS // group_size
    side = GRID * PATCH

    def full_forward(latent_float, cond_float, weights):

        def one_group(operands):
            return group_forward(weights, *operands)
        stacked = (latent_float.reshape(groups, group_size, side, side, CIN), cond_float.reshape(groups, group_size, SEGS, D), segment_ids.reshape(groups, group_size, GRID, GRID), positions.reshape(groups, group_size, GRID, GRID, 2))
        result = lax.map(jax.checkpoint(one_group), stacked)
        return result.reshape(SEQS, side, side, COUT)
    output, pullback = jax.vjp(full_forward, latent.astype(jnp.float32), conditioning.astype(jnp.float32), params)
    grad_latent, grad_conditioning, grad_params = pullback(cotangent.astype(jnp.float32))
    return (output.astype(jnp.bfloat16), grad_latent, grad_conditioning) + tuple(grad_params)
```

```python
from functools import partial
import math

import jax
import jax.numpy as jnp
from jax import lax
from jax.experimental import pallas as pl
from jax.experimental.pallas import tpu as pltpu
from jax.sharding import PartitionSpec as P

HEADS = 16
PATCH = 2
LANES = 128
ROW, COL, SEQ = "row", "col", "seq"
ALL = (ROW, COL, SEQ)
GROUP = (ROW, COL)
F32 = jnp.float32
BF16 = jnp.bfloat16
OUTSIDE = -1e30
VMEM_BYTES = 56 << 20
NN = (((1,), (0,)), ((), ()))
NT = (((1,), (1,)), ((), ()))
TN = (((0,), (0,)), ((), ()))


def mul(left, right, form=NN):
    return lax.dot_general(left, right, form, preferred_element_type=F32)


def attend_body(scale, queries, keys, values, seg_query, seg_key, out, log_total):
    hdim, tokens = queries.shape[1:]
    rate = scale * math.log2(math.e)
    key_side = jnp.concatenate([keys[0], seg_key[...]], axis=0)
    query_side = jnp.concatenate([queries[0], seg_query[...]], axis=0)
    value_side = jnp.concatenate([values[0], jnp.ones((8, tokens), BF16)], axis=0)
    logits = mul(key_side, query_side, TN)
    highest = jnp.max(logits, axis=0, keepdims=True)
    weights = jnp.exp2((logits - highest) * rate)
    summed = mul(value_side, weights.astype(BF16))
    total = summed[hdim : hdim + 1]
    out[0] = (summed[:hdim] / total).astype(BF16)
    log_total[0] = highest * rate + jnp.log2(total)


def attend(qkv, seg_query, seg_key, scale):
    triple, hdim, tokens = qkv.shape
    heads = triple // 3

    def head(offset):
        return pl.BlockSpec((1, hdim, tokens), lambda h: (h + offset, 0, 0))

    whole = pl.BlockSpec((8, tokens), lambda h: (0, 0))
    return pl.pallas_call(
        partial(attend_body, scale),
        grid=(heads,),
        in_specs=[head(0), head(heads), head(2 * heads), whole, whole],
        out_specs=[head(0), pl.BlockSpec((1, 1, tokens), lambda h: (h, 0, 0))],
        out_shape=[
            jax.ShapeDtypeStruct((heads, hdim, tokens), BF16),
            jax.ShapeDtypeStruct((heads, 1, tokens), F32),
        ],
        compiler_params=pltpu.CompilerParams(vmem_limit_bytes=VMEM_BYTES),
        cost_estimate=pl.CostEstimate(
            flops=4 * heads * tokens * tokens * 256,
            bytes_accessed=8 * heads * hdim * tokens,
            transcendentals=heads * tokens * tokens,
        ),
        name="attend",
    )(qkv, qkv, qkv, seg_query, seg_key)


def attend_back_body(
    scale, step, queries, keys, values, out, grad_out, log_total, seg_query, seg_key, gq, gk, gv
):
    hdim, tokens = queries.shape[1:]
    rate = scale * math.log2(math.e)
    query_side = jnp.concatenate([queries[0], seg_query[...]], axis=0)
    grad_t = grad_out[0]
    inner = jnp.sum(grad_t.astype(F32) * out[0].astype(F32), axis=0, keepdims=True)
    total = log_total[0]
    query_rows = queries[0].T
    grad_rows = grad_t.T
    grad_query = jnp.zeros((hdim, tokens), F32)
    for start in range(0, tokens, step):
        part = slice(start, start + step)
        key_part = keys[0, :, part]
        key_side = jnp.concatenate([key_part, seg_key[:, part]], axis=0)
        probability = jnp.exp2(mul(key_side, query_side, TN) * rate - total)
        grad_prob = mul(values[0, :, part], grad_t, TN)
        grad_logits = (probability * (grad_prob - inner)).astype(BF16)
        gv[0, :, part] = mul(probability.astype(BF16), grad_rows).T.astype(BF16)
        gk[0, :, part] = (mul(grad_logits, query_rows) * scale).T.astype(BF16)
        grad_query += mul(key_part, grad_logits)
    gq[0] = (grad_query * scale).astype(BF16)


def attend_back(qkv, out, grad_out, log_total, seg_query, seg_key, scale):
    triple, hdim, tokens = qkv.shape
    heads = triple // 3

    def head(offset):
        return pl.BlockSpec((1, hdim, tokens), lambda h: (h + offset, 0, 0))

    whole = pl.BlockSpec((8, tokens), lambda h: (0, 0))
    return pl.pallas_call(
        partial(attend_back_body, scale, min(tokens, 256)),
        grid=(heads,),
        in_specs=[
            head(0),
            head(heads),
            head(2 * heads),
            head(0),
            head(0),
            pl.BlockSpec((1, 1, tokens), lambda h: (h, 0, 0)),
            whole,
            whole,
        ],
        out_specs=[head(0)] * 3,
        out_shape=[jax.ShapeDtypeStruct((heads, hdim, tokens), BF16)] * 3,
        compiler_params=pltpu.CompilerParams(vmem_limit_bytes=VMEM_BYTES),
        cost_estimate=pl.CostEstimate(
            flops=10 * heads * tokens * tokens * 256,
            bytes_accessed=16 * heads * hdim * tokens,
            transcendentals=heads * tokens * tokens,
        ),
        name="attend_back",
    )(qkv, qkv, qkv, out, grad_out, log_total, seg_query, seg_key)


class Place:
    def __init__(self):
        self.seqs = lax.axis_size(SEQ)
        self.size = (lax.axis_size(ROW), lax.axis_size(COL), self.seqs // 2)
        seq_at = lax.axis_index(SEQ)
        self.at = (lax.axis_index(ROW), lax.axis_index(COL), seq_at // 2)
        self.core = seq_at % 2
        self.chips = self.size[0] * self.size[1] * self.size[2]

    def shift(self, value, axis):
        if axis == 2:
            return lax.ppermute(
                value, SEQ, [(s, (s + 2) % self.seqs) for s in range(self.seqs)]
            )
        count = self.size[axis]
        return lax.ppermute(value, ALL[axis], [(i, (i + 1) % count) for i in range(count)])

    def swap(self, value):
        return lax.ppermute(value, SEQ, [(s, s ^ 1) for s in range(self.seqs)])

    def by_core(self, mine, other, axis):
        low = jnp.concatenate([mine, other], axis=axis)
        high = jnp.concatenate([other, mine], axis=axis)
        return jnp.where(self.core == 0, low, high)


def gather_chips(place, unit, order):
    first, second, third = order
    ring = [unit]
    for _ in range(place.size[first] - 1):
        ring.append(place.shift(ring[-1], first))
    pieces = {(0, 0): jnp.stack(ring)}
    for i in range(1, place.size[second]):
        pieces[(i, 0)] = place.shift(pieces[(i - 1, 0)], second)
    for j in range(1, place.size[third]):
        for i in range(place.size[second]):
            pieces[(i, j)] = place.shift(pieces[(i, j - 1)], third)
    return pieces


def lay_body(size, plans, where, *refs):
    count = sum(2 * len(plan[1]) for plan in plans)
    sources, outs = refs[:count], refs[count:]
    for core in (0, 1):

        def run(core=core):
            at = 0
            for order, keys, targets in plans:
                for half in (core, 1 - core):
                    out, column, width, split = targets[half]
                    for key in keys:
                        spots = [None] * 3
                        for axis, back in zip(order[1:], key):
                            spots[axis] = lax.rem(where[axis] + size[axis] - back, size[axis])
                        chip = spots[1] * size[2] + spots[2]
                        lead = (0, chip) if split is None else (0, chip, split)
                        outs[out][(*lead, slice(None), pl.ds(column, width))] = sources[at][0]
                        at += 1

        pl.when(where[3] == core)(run)


def lay(place, plans, shapes):
    where = jnp.stack([*place.at, place.core]).astype(jnp.int32)
    operands, static = [], []
    for order, mine, other, targets in plans:
        keys = list(mine)
        operands += [mine[k] for k in keys] + [other[k] for k in keys]
        static.append((order, keys, targets))
    rows = place.size[0]

    def piece(value):
        return pl.BlockSpec((1, *value.shape[1:]), lambda k, where: (k, 0, 0))

    def target(shape):
        block = (1, shape[0] // rows, *shape[1:])
        rest = (0,) * len(shape)
        return pl.BlockSpec(block, lambda k, where: (lax.rem(where[0] + rows - k, rows), *rest))

    shapes = [(rows, s[0] // rows, *s[1:]) for s in shapes]
    return pl.pallas_call(
        partial(lay_body, place.size, static),
        grid_spec=pltpu.PrefetchScalarGridSpec(
            num_scalar_prefetch=1,
            grid=(rows,),
            in_specs=[piece(v) for v in operands],
            out_specs=[target((rows * s[1], *s[2:])) for s in shapes],
        ),
        out_shape=[jax.ShapeDtypeStruct(s, BF16) for s in shapes],
        compiler_params=pltpu.CompilerParams(vmem_limit_bytes=VMEM_BYTES),
        cost_estimate=pl.CostEstimate(
            flops=0, transcendentals=0, bytes_accessed=sum(4 * math.prod(s) for s in shapes)
        ),
        name="lay",
    )(where, *operands)


def half_of(value, half, width, axis):
    return lax.dynamic_slice_in_dim(value, half * width, width, axis)


ORDERS = ((0, 1, 2), (0, 2, 1))


def gather_columns(place, shard, widths):
    half = shard.shape[1] // 2
    kept = half_of(shard, place.core, half, 1)
    given = place.swap(half_of(shard, 1 - place.core, half, 1))
    unit = place.by_core(kept, given, 0)
    plans, at = [], 0
    for order, width in zip(ORDERS, widths):
        mine = gather_chips(place, unit[:, at : at + width], order)
        plans.append((order, mine, {k: place.swap(v) for k, v in mine.items()}, at, width))
        at += width
    return plans


def gather_rows(place, shard, widths):
    plans, at = [], 0
    for order, width in zip(ORDERS, widths):
        mine = gather_chips(place, shard[:, at : at + width], order)
        plans.append((order, mine, {k: place.swap(v) for k, v in mine.items()}, at, width))
        at += width
    return plans


def scatter_chips(place, blocks, order):
    names = [0, 1, 2]
    for axis in reversed(order):
        spot = names.index(axis)
        count, at = place.size[axis], place.at[axis]

        def block(back):
            index = lax.rem(at + 2 * count - back, count)
            return lax.dynamic_index_in_dim(blocks, index, spot, keepdims=False)

        total = block(1)
        for step in range(2, count + 1):
            total = (
                place.shift(total, axis).astype(F32) + block(step).astype(F32)
            ).astype(BF16)
        blocks = total
        names.remove(axis)
    return blocks


def two_way(width):
    low = width // (2 * LANES) * LANES
    return (low, width - low) if low else (width,)


def scatter_columns(place, lhs, rhs, orders):
    half = rhs.shape[1] // 2
    grid = (*place.size, lhs.shape[1] // place.chips, half)
    sent = place.swap(mul(lhs, half_of(rhs, 1 - place.core, half, 1), TN).astype(BF16))
    kept = mul(lhs, half_of(rhs, place.core, half, 1), TN)
    blocks = (kept + sent.astype(F32)).astype(BF16).reshape(grid)
    return finish_columns(place, blocks, orders)


def finish_columns(place, blocks, orders):
    parts, at = [], 0
    widths = two_way(blocks.shape[-1]) if len(orders) == 2 else (blocks.shape[-1],)
    for order, width in zip(orders, widths):
        parts.append(scatter_chips(place, blocks[..., at : at + width], order))
        at += width
    total = jnp.concatenate(parts, axis=1)
    rows = total.shape[0] // 2
    mine = half_of(total, place.core, rows, 0)
    other = place.swap(half_of(total, 1 - place.core, rows, 0))
    return place.by_core(mine, other, 1).astype(F32)


def scatter_rows(place, full):
    rows = full.shape[0] // (2 * place.chips)
    blocks = full.reshape(*place.size, 2, rows, full.shape[1])
    sent = place.swap(lax.dynamic_index_in_dim(blocks, 1 - place.core, 3, keepdims=False))
    kept = lax.dynamic_index_in_dim(blocks, place.core, 3, keepdims=False)
    blocks = (kept.astype(F32) + sent.astype(F32)).astype(BF16)
    parts, at = [], 0
    for order, width in zip(ORDERS, two_way(full.shape[1])):
        parts.append(scatter_chips(place, blocks[..., at : at + width], order))
        at += width
    return jnp.concatenate(parts, axis=1).astype(F32)


def normalise(stream):
    average = jnp.mean(stream, axis=-1, keepdims=True)
    centred = stream - average
    rate = lax.rsqrt(jnp.mean(centred * centred, axis=-1, keepdims=True) + 1e-06)
    return centred * rate, rate


def normalise_back(grad, scale, xhat, rate):
    inner = grad * (1.0 + scale)
    first = jnp.mean(inner, axis=-1, keepdims=True)
    second = jnp.mean(inner * xhat, axis=-1, keepdims=True)
    return rate * (inner - first - xhat * second)


def gelu_pair(pre):
    rate = math.sqrt(2.0 / math.pi)
    square = pre * pre
    bend = jnp.tanh(rate * pre * (1.0 + 0.044715 * square))
    half = 0.5 * (1.0 + bend)
    slope = half + 0.5 * pre * (1.0 - bend * bend) * rate * (1.0 + 3 * 0.044715 * square)
    return pre * half, slope


def split_high(value):
    high = value.astype(BF16)
    return high, (value - high.astype(F32)).astype(BF16)


def block_tokens(grid, rows, cols):
    seqs, channels = grid.shape[0], grid.shape[-1]
    parts = grid.reshape(seqs, rows, PATCH, cols, PATCH, channels).transpose(0, 2, 4, 5, 1, 3)
    return parts.reshape(seqs, PATCH * PATCH * channels, rows * cols)


def unblock_tokens(parts, rows, cols):
    seqs = parts.shape[0]
    channels = parts.shape[1] // (PATCH * PATCH)
    grid = parts.reshape(seqs, PATCH, PATCH, channels, rows, cols).transpose(0, 4, 1, 5, 2, 3)
    return grid.reshape(seqs, rows * PATCH, cols * PATCH, channels)


def per_device(
    latent,
    conditioning,
    segment_ids,
    positions,
    cotangent,
    w_embed,
    b_embed,
    w_mod,
    b_mod,
    w_qkv,
    b_query,
    b_value,
    w_proj,
    b_proj,
    w_up,
    b_up,
    w_down,
    b_down,
    w_final_mod,
    b_final_mod,
    w_out,
    b_out,
):
    place = Place()
    devices = 2 * place.chips
    rows_all, cols_all = place.size[0], place.size[1]
    group = rows_all * cols_all
    seqs_here, grid_side = segment_ids.shape[:2]
    rows_here, cols_here = latent.shape[1] // PATCH, latent.shape[2] // PATCH
    spot = rows_here * cols_here
    tokens = group * spot
    width = w_embed.shape[1]
    hidden = b_up.shape[0] * devices
    crops = conditioning.shape[1]
    unit = width // devices
    me = (place.at[0] * cols_all + place.at[1]) * place.seqs + lax.axis_index(SEQ)
    slot = place.at[0] * cols_all + place.at[1]
    mine = jnp.minimum(slot, seqs_here - 1)
    active = slot < seqs_here
    whose = jnp.minimum(jnp.arange(group), seqs_here - 1)

    packed = jnp.concatenate(
        [
            block_tokens(latent, rows_here, cols_here),
            block_tokens(cotangent, rows_here, cols_here),
            positions.reshape(seqs_here, spot, 2).transpose(0, 2, 1).astype(BF16),
        ],
        axis=1,
    )
    packed = jnp.concatenate([packed, *[packed[-1:]] * (group - seqs_here)], axis=0)
    packed = lax.all_to_all(packed, GROUP, 0, 0, tiled=True)
    packed = packed.transpose(1, 0, 2).reshape(-1, tokens)
    p_in = w_embed.shape[0]
    p_out = b_out.shape[0]
    patches_t = packed[:p_in]
    grad_tokens_t = jnp.where(active, packed[p_in : p_in + p_out], 0)
    place_row, place_col = packed[p_in + p_out], packed[p_in + p_out + 1]
    seg = lax.dynamic_index_in_dim(segment_ids, mine, 0, keepdims=False)
    seg = seg.reshape(rows_all, rows_here, cols_all, cols_here).transpose(0, 2, 1, 3)
    seg = seg.reshape(tokens)
    seg_hot = seg[None, :] == jnp.arange(8, dtype=jnp.int32)[:, None]
    seg_key = seg_hot.astype(BF16)
    real_crop = jnp.arange(8)[:, None] < crops
    seg_query = jnp.where(seg_hot | ~real_crop, 0.0, OUTSIDE).astype(BF16)
    seg_col = seg[:, None]

    first = gather_columns(place, jnp.concatenate([w_qkv, w_proj], axis=1), (width, width))
    second = gather_columns(place, w_up, two_way(hidden // 2))
    third = gather_rows(place, w_down, two_way(width))

    share = -(-seqs_here * crops // group)
    cond_f32 = conditioning.astype(F32).reshape(seqs_here * crops, width)
    sigmoid = jax.nn.sigmoid(cond_f32)
    cond_low = (cond_f32 * sigmoid).astype(BF16)
    cond_padded = jnp.pad(cond_low, ((0, share * group - seqs_here * crops), (0, 0)))
    cond_share = lax.dynamic_slice_in_dim(cond_padded, slot * share, share, 0)
    small = [b_query, b_value, b_proj, b_down, b_embed, b_up, w_out.reshape(-1), cond_share.reshape(-1)]
    sizes = [s.shape[0] for s in small]
    small = lax.all_gather(jnp.concatenate(small)[None], ALL, axis=0, tiled=True)
    parts, at = [], 0
    for size in sizes:
        parts.append(small[:, at : at + size])
        at += size
    query_bias, value_bias, proj_bias, down_bias, embed_bias, up_bias = [
        p.reshape(-1) for p in parts[:6]
    ]
    out_full = parts[6].reshape(width, p_out)
    cond_all = parts[7].reshape(group, place.seqs, share, width).transpose(1, 0, 2, 3)
    cond_all = cond_all.reshape(place.seqs, share * group, width)[:, : seqs_here * crops]
    cond_all = cond_all.reshape(-1, width)

    mod_cols, fin_cols = b_mod.shape[0], b_final_mod.shape[0]
    mod_share = jnp.concatenate(
        [
            w_mod.reshape(unit, devices, mod_cols).transpose(1, 0, 2),
            w_final_mod.reshape(unit, devices, fin_cols).transpose(1, 0, 2),
        ],
        axis=2,
    )
    mod_share = lax.all_to_all(mod_share, ALL, 0, 0, tiled=True).reshape(width, -1)
    mod_bias = jnp.concatenate([b_mod, b_final_mod]).astype(F32)
    mod_rows = (mul(cond_all, mod_share) + mod_bias).reshape(
        place.seqs, seqs_here, crops, mod_cols + fin_cols
    )
    mod_rows = jnp.concatenate([mod_rows, *[mod_rows[:, -1:]] * (group - seqs_here)], axis=1)
    mod_rows = mod_rows.transpose(1, 0, 2, 3).reshape(devices, crops, -1)
    mod_rows = lax.all_to_all(mod_rows, ALL, 0, 0, tiled=True).transpose(1, 0, 2)
    modulation = jnp.concatenate(
        [
            mod_rows[..., :mod_cols].reshape(crops, -1),
            mod_rows[..., mod_cols:].reshape(crops, -1),
        ],
        axis=1,
    )

    def by_crop(piece):
        rows = modulation[:, piece * width : (piece + 1) * width]
        value = rows[crops - 1 :]
        for g in range(crops - 1):
            value = jnp.where(seg_col == g, rows[g : g + 1], value)
        return value

    shift_one, scale_one, gate_one, shift_two, scale_two, gate_two, shift_three, scale_three = [
        by_crop(i) for i in range(8)
    ]

    def crop_sum(value):
        return mul(seg_key, value.astype(BF16))[:crops]

    quarter = width // 4
    frequency = jnp.exp(jnp.arange(quarter, dtype=F32) / quarter * -math.log(10000.0))
    angle = jnp.arange(grid_side, dtype=F32)[:, None] * frequency
    table_high, table_low = split_high(jnp.concatenate([jnp.sin(angle), jnp.cos(angle)], axis=1))
    blank = jnp.zeros_like(table_high)
    steps = jnp.arange(grid_side, dtype=F32).astype(BF16)[:, None]
    row_hot = (place_row[None] == steps).astype(BF16)
    col_hot = (place_col[None] == steps).astype(BF16)
    embed_lhs = jnp.concatenate(
        [patches_t, row_hot, col_hot, row_hot, col_hot, jnp.ones((16, tokens), BF16)], axis=0
    )
    embed_rhs = jnp.concatenate(
        [
            w_embed,
            jnp.concatenate([table_high, blank], axis=1),
            jnp.concatenate([blank, table_high], axis=1),
            jnp.concatenate([table_low, blank], axis=1),
            jnp.concatenate([blank, table_low], axis=1),
            embed_bias[None],
            jnp.zeros((15, width), BF16),
        ],
        axis=0,
    )
    embedded = mul(embed_lhs, embed_rhs, TN)

    targets = []
    for _, _, _, at, wide in first:
        spots = []
        for half in (0, 1):
            column = half * 2 * width + at
            spots.append((0, column, wide, None) if column < 3 * width else (1, column - 3 * width, wide, None))
        targets.append(spots)
    qkv_full, proj_full = lay(
        place,
        [(o, a, b, t) for (o, a, b, _, _), t in zip(first, targets)],
        [(place.chips, 2 * unit, 3 * width), (place.chips, 2 * unit, width)],
    )
    qkv_full, proj_full = qkv_full.reshape(width, 3 * width), proj_full.reshape(width, width)
    (up_full,) = lay(
        place,
        [
            (o, a, b, [(0, h * hidden // 2 + at, wide, None) for h in (0, 1)])
            for o, a, b, at, wide in second
        ],
        [(place.chips, 2 * unit, hidden)],
    )
    up_full = up_full.reshape(width, hidden)
    (down_full,) = lay(
        place,
        [(o, a, b, [(0, at, wide, h) for h in (0, 1)]) for o, a, b, at, wide in third],
        [(place.chips, 2, w_down.shape[0], width)],
    )
    down_full = down_full.reshape(hidden, width)

    xhat_one, rate_one = normalise(embedded)
    hidden_one = (xhat_one * (1.0 + scale_one) + shift_one).astype(BF16)
    qkv_bias = jnp.concatenate([query_bias, jnp.zeros_like(query_bias), value_bias]).astype(F32)
    qkv = (mul(qkv_full, hidden_one, (((0,), (1,)), ((), ()))) + qkv_bias[:, None]).astype(BF16)
    hdim = width // HEADS
    qkv = qkv.reshape(3 * HEADS, hdim, tokens)
    score_scale = 1.0 / math.sqrt(hdim)
    attended, log_total = attend(qkv, seg_query, seg_key, score_scale)
    attended_t = attended.reshape(width, tokens)
    projected = mul(attended_t, proj_full, TN) + proj_bias.astype(F32)
    mixed_one = embedded + gate_one * projected
    xhat_two, rate_two = normalise(mixed_one)
    hidden_two = (xhat_two * (1.0 + scale_two) + shift_two).astype(BF16)
    activated, slope = gelu_pair(mul(hidden_two, up_full) + up_bias.astype(F32))
    activated, slope = activated.astype(BF16), slope.astype(BF16)
    mlp_out = mul(activated, down_full) + down_bias.astype(F32)
    mixed_two = mixed_one + gate_two * mlp_out
    xhat_three, rate_three = normalise(mixed_two)
    hidden_three = (xhat_three * (1.0 + scale_three) + shift_three).astype(BF16)
    token_out_t = mul(out_full, hidden_three, (((0,), (1,)), ((), ()))) + b_out.astype(F32)[:, None]

    grad_hidden_three = mul(grad_tokens_t, out_full, (((0,), (1,)), ((), ())))
    grad_mixed_two = normalise_back(grad_hidden_three, scale_three, xhat_three, rate_three)
    grad_mlp = (grad_mixed_two * gate_two).astype(BF16)
    shard_down = scatter_rows(place, mul(activated, grad_mlp, TN).astype(BF16))
    grad_pre = (slope.astype(F32) * mul(grad_mlp, down_full, NT)).astype(BF16)
    shard_up = scatter_columns(place, hidden_two, grad_pre, ORDERS)
    grad_hidden_two = mul(grad_pre, up_full, NT)
    grad_mixed_one = grad_mixed_two + normalise_back(grad_hidden_two, scale_two, xhat_two, rate_two)
    grad_proj = (grad_mixed_one * gate_one).astype(BF16)
    grad_w_proj = mul(attended_t, grad_proj)
    grad_w_out = mul(hidden_three, grad_tokens_t, (((0,), (1,)), ((), ())))
    both = jnp.concatenate(
        [grad_w_proj, jnp.pad(grad_w_out, ((0, 0), (0, LANES - p_out)))], axis=1
    ).astype(BF16)
    half = both.shape[1] // 2
    kept = half_of(both, place.core, half, 1).astype(F32)
    kept = kept + place.swap(half_of(both, 1 - place.core, half, 1)).astype(F32)
    kept = kept.astype(BF16).reshape(*place.size, 2 * unit, half)
    shard_both = finish_columns(place, kept, ORDERS[:1])
    shard_proj, shard_out = shard_both[:, :width], shard_both[:, width : width + p_out]
    grad_attended = mul(proj_full, grad_proj, NT).astype(BF16)
    grad_queries, grad_keys, grad_values = attend_back(
        qkv,
        attended,
        grad_attended.reshape(HEADS, hdim, tokens),
        log_total,
        seg_query,
        seg_key,
        score_scale,
    )
    grad_qkv_t = jnp.concatenate([grad_queries, grad_keys, grad_values], axis=0)
    grad_qkv_t = grad_qkv_t.reshape(3 * width, tokens)
    wide = -(-3 * width // (2 * LANES)) * 2 * LANES
    padded = jnp.pad(grad_qkv_t, ((0, wide - 3 * width), (0, 0)))
    half = wide // 2
    sent = mul(hidden_one, half_of(padded, 1 - place.core, half, 0), (((0,), (1,)), ((), ())))
    sent = place.swap(sent.astype(BF16))
    kept = mul(hidden_one, half_of(padded, place.core, half, 0), (((0,), (1,)), ((), ())))
    blocks = (kept + sent.astype(F32)).astype(BF16).reshape(*place.size, 2 * unit, half)
    shard_qkv = finish_columns(place, blocks, ORDERS)[:, : 3 * width]
    grad_hidden_one = mul(grad_qkv_t, qkv_full, (((0,), (1,)), ((), ())))
    grad_embedded = grad_mixed_one + normalise_back(
        grad_hidden_one, scale_one, xhat_one, rate_one
    )
    grad_embedded_low = grad_embedded.astype(BF16)
    grad_w_embed = mul(patches_t, grad_embedded_low)
    grad_b_embed = jnp.sum(grad_embedded, axis=0)
    grad_patches_t = mul(w_embed, grad_embedded_low, NT)

    grad_mod = jnp.concatenate(
        [
            crop_sum(grad_hidden_one),
            crop_sum(grad_hidden_one * xhat_one),
            crop_sum(grad_mixed_one * projected),
            crop_sum(grad_hidden_two),
            crop_sum(grad_hidden_two * xhat_two),
            crop_sum(grad_mixed_two * mlp_out),
            crop_sum(grad_hidden_three),
            crop_sum(grad_hidden_three * xhat_three),
        ],
        axis=1,
    ).astype(BF16)
    grad_mod = lax.all_gather(grad_mod[None], ALL, axis=0, tiled=True)
    grad_mod = grad_mod.reshape(group, place.seqs, crops, 8 * width)[:seqs_here]
    grad_mod = grad_mod.transpose(1, 0, 2, 3).reshape(-1, 8 * width)
    cond_mine = lax.dynamic_slice_in_dim(cond_all, me * unit, unit, 1)
    shard_all_mod = mul(cond_mine, grad_mod, TN)
    shard_mod, shard_final = shard_all_mod[:, : 6 * width], shard_all_mod[:, 6 * width :]
    bias_mod = lax.dynamic_slice_in_dim(grad_mod[:, : 6 * width], me * mod_cols, mod_cols, 1)
    bias_mod = jnp.sum(bias_mod.astype(F32), axis=0)
    bias_final = lax.dynamic_slice_in_dim(grad_mod[:, 6 * width :], me * fin_cols, fin_cols, 1)
    bias_final = jnp.sum(bias_final.astype(F32), axis=0)
    grad_cond = mul(grad_mod, jnp.concatenate([w_mod, w_final_mod], axis=1), NT)
    grad_cond = grad_cond.reshape(place.seqs, seqs_here * crops, unit)
    grad_cond = jnp.broadcast_to(grad_cond[None], (group, *grad_cond.shape))
    grad_cond = grad_cond.reshape(devices, seqs_here * crops, unit)
    grad_cond = lax.all_to_all(grad_cond, ALL, 0, 0, tiled=True)
    grad_cond = grad_cond.transpose(1, 0, 2).reshape(seqs_here * crops, width)
    grad_cond = grad_cond * (sigmoid * (1.0 + cond_f32 * (1.0 - sigmoid)))
    grad_conditioning = grad_cond.reshape(seqs_here, crops, width)

    grad_qkv_sum = jnp.sum(grad_qkv_t.astype(F32), axis=1)
    sums = [
        grad_b_embed,
        grad_qkv_sum[:width],
        grad_qkv_sum[2 * width :],
        jnp.sum(grad_proj.astype(F32), axis=0),
        jnp.sum(grad_mlp.astype(F32), axis=0),
        jnp.sum(grad_pre.astype(F32), axis=0),
    ]
    sums = jnp.concatenate([s.reshape(devices, -1) for s in sums], axis=1)
    sums = jnp.sum(lax.all_to_all(sums, ALL, 0, 0, tiled=True), axis=0)
    shard_biases = [sums[i * unit : (i + 1) * unit] for i in range(5)] + [sums[5 * unit :]]
    grad_b_out = jnp.sum(grad_tokens_t.astype(F32), axis=1)
    small_w_embed, small_b_out = lax.psum((grad_w_embed, grad_b_out), ALL)

    back = jnp.concatenate([token_out_t, grad_patches_t], axis=0)
    back = back.reshape(-1, group, spot).transpose(1, 0, 2)
    back = lax.all_to_all(back, GROUP, 0, 0, tiled=True)[:seqs_here]
    prediction = unblock_tokens(back[:, :p_out].astype(BF16), rows_here, cols_here)
    grad_latent = unblock_tokens(back[:, p_out:], rows_here, cols_here)
    return (
        prediction,
        grad_latent,
        grad_conditioning,
        small_w_embed,
        shard_biases[0],
        shard_mod,
        bias_mod,
        shard_qkv,
        shard_biases[1],
        shard_biases[2],
        shard_proj,
        shard_biases[3],
        shard_up,
        shard_biases[5],
        shard_down,
        shard_biases[4],
        shard_final,
        bias_final,
        shard_out,
        small_b_out,
    )


def solution(mesh):
    grid, seqs, split, rows = P(SEQ, ROW, COL, None), P(SEQ, None, None), P(ALL), P(ALL, None)
    in_specs = (grid, seqs, seqs, grid, grid, P(), split, rows, split, rows, split, split)
    in_specs += (rows, split, rows, split, rows, split, rows, split, rows, P())
    out_specs = (grid, grid, seqs, P(), split, rows, split, rows, split, split)
    out_specs += (rows, split, rows, split, rows, split, rows, split, rows, P())
    return jax.shard_map(
        per_device, mesh=mesh, in_specs=in_specs, out_specs=out_specs, check_vma=False
    )
```

```python
from functools import partial
import math

import jax
import jax.numpy as jnp
from jax import lax
from jax.experimental import pallas as pl
from jax.experimental.pallas import tpu as pltpu
from jax.sharding import PartitionSpec as P

HEADS = 16
PATCH = 2
LANES = 128
ROW, COL, SEQ = "row", "col", "seq"
ALL = (ROW, COL, SEQ)
GROUP = (ROW, COL)
F32 = jnp.float32
BF16 = jnp.bfloat16
OUTSIDE = -1e30
VMEM_BYTES = 56 << 20
BRIEF = pl.CostEstimate(flops=1, bytes_accessed=1, transcendentals=0)
NN = (((1,), (0,)), ((), ()))
NT = (((1,), (1,)), ((), ()))
TN = (((0,), (0,)), ((), ()))


def mul(left, right, form=NN):
    return lax.dot_general(left, right, form, preferred_element_type=F32)


def attend_body(scale, queries, keys, values, seg_query, seg_key, *rest):
    out, log_total = rest[-2:]
    hdim, tokens = queries.shape[1:]
    rate = scale * math.log2(math.e)
    key_side = jnp.concatenate([keys[0], seg_key[...]], axis=0)
    query_side = jnp.concatenate([queries[0], seg_query[...]], axis=0)
    value_side = jnp.concatenate([values[0], jnp.ones((8, tokens), BF16)], axis=0)
    logits = mul(key_side, query_side, TN)
    highest = jnp.max(logits, axis=0, keepdims=True)
    weights = jnp.exp2((logits - highest) * rate)
    summed = mul(value_side, weights.astype(BF16))
    total = summed[hdim : hdim + 1]
    out[0] = (summed[:hdim] / total).astype(BF16)
    log_total[0] = highest * rate + jnp.log2(total)


def attend(qkv, seg_query, seg_key, scale, first, count, into=()):
    triple, hdim, tokens = qkv.shape
    heads = triple // 3

    def head(offset):
        return pl.BlockSpec((1, hdim, tokens), lambda h: (h + offset + first, 0, 0))

    whole = pl.BlockSpec((8, tokens), lambda h: (0, 0))
    return pl.pallas_call(
        partial(attend_body, scale),
        grid=(count,),
        in_specs=[head(0), head(heads), head(2 * heads), whole, whole]
        + [pl.BlockSpec(memory_space=pl.ANY)] * len(into),
        out_specs=[head(0), pl.BlockSpec((1, 1, tokens), lambda h: (h + first, 0, 0))],
        out_shape=[
            jax.ShapeDtypeStruct((heads, hdim, tokens), BF16),
            jax.ShapeDtypeStruct((heads, 1, tokens), F32),
        ],
        input_output_aliases={5 + n: n for n in range(len(into))},
        compiler_params=pltpu.CompilerParams(vmem_limit_bytes=VMEM_BYTES),
        cost_estimate=BRIEF,
        name="attend",
    )(qkv, qkv, qkv, seg_query, seg_key, *into)


def attend_back_body(
    scale, step, queries, keys, values, out, grad_out, log_total, seg_query, seg_key, *rest
):
    grads = rest[-1]
    hdim, tokens = queries.shape[1:]
    rate = scale * math.log2(math.e)
    query_side = jnp.concatenate([queries[0], seg_query[...]], axis=0)
    grad_t = grad_out[0]
    inner = jnp.sum(grad_t.astype(F32) * out[0].astype(F32), axis=0, keepdims=True)
    total = log_total[0]
    query_rows = queries[0].T
    grad_rows = grad_t.T
    grad_query = jnp.zeros((hdim, tokens), F32)
    for start in range(0, tokens, step):
        part = slice(start, start + step)
        key_part = keys[0, :, part]
        key_side = jnp.concatenate([key_part, seg_key[:, part]], axis=0)
        probability = jnp.exp2(mul(key_side, query_side, TN) * rate - total)
        grad_prob = mul(values[0, :, part], grad_t, TN)
        grad_logits = (probability * (grad_prob - inner)).astype(BF16)
        grads[2, 0, :, part] = mul(probability.astype(BF16), grad_rows).T.astype(BF16)
        grads[1, 0, :, part] = (mul(grad_logits, query_rows) * scale).T.astype(BF16)
        grad_query += mul(key_part, grad_logits)
    grads[0, 0] = (grad_query * scale).astype(BF16)


def attend_back(qkv, out, grad_out, log_total, seg_query, seg_key, scale, first, count, into=None):
    triple, hdim, tokens = qkv.shape
    heads = triple // 3

    def head(offset):
        return pl.BlockSpec((1, hdim, tokens), lambda h: (h + offset + first, 0, 0))

    whole = pl.BlockSpec((8, tokens), lambda h: (0, 0))
    given = [] if into is None else [into]
    return pl.pallas_call(
        partial(attend_back_body, scale, min(tokens, 256)),
        grid=(count,),
        in_specs=[
            head(0),
            head(heads),
            head(2 * heads),
            head(0),
            head(0),
            pl.BlockSpec((1, 1, tokens), lambda h: (h + first, 0, 0)),
            whole,
            whole,
        ]
        + [pl.BlockSpec(memory_space=pl.ANY)] * len(given),
        out_specs=pl.BlockSpec((3, 1, hdim, tokens), lambda h: (0, h + first, 0, 0)),
        out_shape=jax.ShapeDtypeStruct((3, heads, hdim, tokens), BF16),
        input_output_aliases={8: 0} if given else {},
        compiler_params=pltpu.CompilerParams(vmem_limit_bytes=VMEM_BYTES),
        cost_estimate=BRIEF,
        name="attend_back",
    )(qkv, qkv, qkv, out, grad_out, log_total, seg_query, seg_key, *given)


class Place:
    def __init__(self):
        self.seqs = lax.axis_size(SEQ)
        self.size = (lax.axis_size(ROW), lax.axis_size(COL), self.seqs // 2)
        seq_at = lax.axis_index(SEQ)
        self.at = (lax.axis_index(ROW), lax.axis_index(COL), seq_at // 2)
        self.core = seq_at % 2
        self.chips = self.size[0] * self.size[1] * self.size[2]

    def shift(self, value, axis, steps=1):
        if axis == 2:
            return lax.ppermute(
                value, SEQ, [(s, (s + 2 * steps) % self.seqs) for s in range(self.seqs)]
            )
        count = self.size[axis]
        return lax.ppermute(value, ALL[axis], [(i, (i + steps) % count) for i in range(count)])

    def swap(self, value):
        return lax.ppermute(value, SEQ, [(s, s ^ 1) for s in range(self.seqs)])

    def mover(self, axis, steps=1):
        return lambda value: self.shift(value, axis, steps)

    def by_core(self, mine, other, axis):
        low = jnp.concatenate([mine, other], axis=axis)
        high = jnp.concatenate([other, mine], axis=axis)
        return jnp.where(self.core == 0, low, high)


class Chain:
    def __init__(self, stages):
        self.stages = stages
        self.result = None
        self.flying = None
        self.ready = next(stages)
        self.launch([value for value, _ in self.ready])

    def launch(self, values):
        self.flying = [move(value) for value, (_, move) in zip(values, self.ready)]
        self.ready = None

    def land(self, came):
        self.flying = None
        try:
            self.ready = self.stages.send(came)
        except StopIteration as end:
            self.result = end.value


def step(chains, *work):
    chains = [c for c in chains if c.flying is not None]
    came, work = lax.optimization_barrier(([c.flying for c in chains], work))
    for chain, values in zip(chains, came):
        chain.land(values)
    going = [c for c in chains if c.ready is not None]
    values, work = lax.optimization_barrier(
        ([[value for value, _ in c.ready] for c in going], work)
    )
    for chain, sent in zip(going, values):
        chain.launch(sent)
    return work[0] if len(work) == 1 else work


def finish(chain):
    while chain.flying is not None:
        chain.land(chain.flying)
        if chain.ready is not None:
            chain.launch([value for value, _ in chain.ready])
    return chain.result


def one_move(value, move):
    (came,) = yield [(value, move)]
    return came


def gather_seqs(place, value):
    xs, x_at = place.size[2], place.at[2]
    (other,) = yield [(value, place.swap)]
    pair = place.by_core(value[None], other[None], 0)
    came = yield [(pair, place.mover(2, back)) for back in range(1, xs)]
    ring = jnp.stack([*came[::-1], pair] * 2)
    ring = lax.dynamic_slice_in_dim(ring, xs - 1 - x_at, xs, 0)
    return ring.reshape(place.seqs, *value.shape)


def gather_chips(place, unit, low, ring=True):
    rows, cols, xs = place.size
    if ring:
        column = [unit]
        for _ in range(1, rows):
            column += yield [(column[-1], place.mover(0))]
    else:
        column = [unit, *(yield [(unit, place.mover(0, back)) for back in range(1, rows)])]
    pieces = {(0, 0): [(0, jnp.stack(column))]}
    swapped = []

    def swaps():
        return [(v, place.swap) for _, v in list_all()[len(swapped) :]]

    def list_all():
        return [((key, at), value) for key, parts in pieces.items() for at, value in parts]

    by_col, by_x = pieces[0, 0][0][1], pieces[0, 0][0][1]
    for hop in range(1, max(cols, xs)):
        going = []
        if hop < cols:
            going.append((by_col, place.mover(1)))
        if hop < xs:
            going.append((by_x, place.mover(2)))
        came = yield going + swaps()
        swapped += came[len(going) :]
        if hop < cols:
            by_col = came[0]
            pieces[hop, 0] = [(0, by_col)]
        if hop < xs:
            by_x = came[len(going) - 1]
            pieces[0, hop] = [(0, by_x)]

    def columns(key, first):
        parts = pieces[key]
        if len(parts) == 2:
            return parts[0 if first else 1][1]
        return parts[0][1][..., :low] if first else parts[0][1][..., low:]

    for total in range(2, cols + xs - 1):
        todo = [(i, total - i) for i in range(1, cols) if 1 <= total - i < xs]
        going = []
        for i, j in todo:
            going.append((columns((i, j - 1), True), place.mover(2)))
            going.append((columns((i - 1, j), False), place.mover(1)))
        came = yield going + swaps()
        swapped += came[len(going) :]
        for n, key in enumerate(todo):
            pieces[key] = [(0, came[2 * n]), (low, came[2 * n + 1])]
    swapped += yield swaps()
    mine = [(key, at, value) for (key, at), value in list_all()]
    other = [(key, at, value) for (key, at, _), value in zip(mine, swapped)]
    return [(0, *p) for p in mine] + [(1, *p) for p in other]


def lay_body(size, static, targets, where, *refs):
    sources, outs = refs[: len(static)], refs[len(static) :]
    for core in (0, 1):

        def run(core=core):
            for ref, (side, key, at, width) in zip(sources, static):
                spots = [
                    lax.rem(where[axis + 1] + size[axis + 1] - back, size[axis + 1])
                    for axis, back in enumerate(key)
                ]
                chip = spots[0] * size[2] + spots[1]
                for out, start, column, wide, split in targets[core if side == 0 else 1 - core]:
                    low, high = max(at, start), min(at + width, start + wide)
                    if low < high:
                        lead = (0, chip) if split is None else (0, chip, split)
                        spot = pl.ds(column + low - start, high - low)
                        outs[out][(*lead, slice(None), spot)] = ref[0, :, low - at : high - at]

        pl.when(where[3] == core)(run)


def lay(place, pieces, targets, shapes):
    where = jnp.stack([*place.at, place.core]).astype(jnp.int32)
    static = [(side, key, at, value.shape[-1]) for side, key, at, value in pieces]
    operands = [p[3] for p in pieces]
    rows = place.size[0]

    def piece(value):
        return pl.BlockSpec((1, *value.shape[1:]), lambda k, where: (k, 0, 0))

    def target(shape):
        rest = (0,) * (len(shape) - 1)
        return pl.BlockSpec(
            (1, *shape[1:]), lambda k, where: (lax.rem(where[0] + rows - k, rows), *rest)
        )

    shapes = [(rows, s[0] // rows, *s[1:]) for s in shapes]
    return pl.pallas_call(
        partial(lay_body, place.size, static, targets),
        grid_spec=pltpu.PrefetchScalarGridSpec(
            num_scalar_prefetch=1,
            grid=(rows,),
            in_specs=[piece(v) for v in operands],
            out_specs=[target(s) for s in shapes],
        ),
        out_shape=[jax.ShapeDtypeStruct(s, BF16) for s in shapes],
        compiler_params=pltpu.CompilerParams(vmem_limit_bytes=VMEM_BYTES),
        cost_estimate=BRIEF,
        name="lay",
    )(where, *operands)


def half_of(value, half, width, axis):
    return lax.dynamic_slice_in_dim(value, half * width, width, axis)


def lower_half(width):
    return width // (2 * LANES) * LANES


def gather_columns(place, shard, ring=True):
    half = shard.shape[1] // 2
    kept = half_of(shard, place.core, half, 1)
    (given,) = yield [(half_of(shard, 1 - place.core, half, 1), place.swap)]
    return (yield from gather_chips(place, place.by_core(kept, given, 0), lower_half(half), ring))


def block_of(blocks, axis, at):
    return lax.dynamic_index_in_dim(blocks, at, axis, keepdims=False)


def plus(*terms):
    return sum(t.astype(F32) for t in terms)


def scatter_chips(place, blocks):
    rows, cols, xs = place.size
    row_at, col_at, x_at = place.at
    if (cols, xs) == (2, 2):
        low = lower_half(blocks.shape[-1])
        by_col, by_x = block_of(blocks, 1, 1 - col_at), block_of(blocks, 1, col_at)
        far, by_col = block_of(by_col, 1, 1 - x_at), block_of(by_col, 1, x_at)
        own, by_x = block_of(by_x, 1, x_at), block_of(by_x, 1, 1 - x_at)
        far_x, far_col = yield [(far[..., :low], place.mover(2)), (far[..., low:], place.mover(1))]
        by_col = jnp.concatenate(
            [plus(by_col[..., :low], far_x).astype(BF16), by_col[..., low:]], axis=-1
        )
        by_x = jnp.concatenate(
            [by_x[..., :low], plus(by_x[..., low:], far_col).astype(BF16)], axis=-1
        )
        from_col, from_x = yield [(by_col, place.mover(1)), (by_x, place.mover(2))]
        own = plus(own, from_col, from_x).astype(BF16)
    else:
        own = blocks
        for axis, spot, count, at in ((2, 2, xs, x_at), (1, 1, cols, col_at)):
            total = block_of(own, spot, lax.rem(at + count - 1, count))
            for back in range(2, count + 1):
                here = block_of(own, spot, lax.rem(at + 2 * count - back, count))
                (given,) = yield [(total, place.mover(axis))]
                total = plus(given, here).astype(BF16)
            own = total
    given = yield [
        (block_of(own, 0, lax.rem(row_at + back, rows)), place.mover(0, back))
        for back in range(1, rows)
    ]
    return plus(block_of(own, 0, row_at), *given)


def finish_columns(place, blocks):
    total = yield from scatter_chips(place, blocks.reshape(*place.size, -1, blocks.shape[1]))
    rows = total.shape[0] // 2
    mine = half_of(total, place.core, rows, 0)
    (other,) = yield [(half_of(total, 1 - place.core, rows, 0), place.swap)]
    return place.by_core(mine, other, 1)


def scatter_rows(place, kept, sent):
    (sent,) = yield [(sent, place.swap)]
    blocks = plus(kept, sent).astype(BF16)
    return (yield from scatter_chips(place, blocks.reshape(*place.size, *kept.shape[1:])))


def exchange(value, axes=ALL):
    return lax.all_to_all(value, axes, 0, 0, tiled=True)


def for_all(value, devices):
    return jnp.broadcast_to(value[None], (devices, *value.shape))


def normalise(stream):
    average = jnp.mean(stream, axis=-1, keepdims=True)
    centred = stream - average
    rate = lax.rsqrt(jnp.mean(centred * centred, axis=-1, keepdims=True) + 1e-06)
    return centred * rate, rate


def normalise_back(grad, scale, xhat, rate):
    inner = grad * (1.0 + scale)
    first = jnp.mean(inner, axis=-1, keepdims=True)
    second = jnp.mean(inner * xhat, axis=-1, keepdims=True)
    return rate * (inner - first - xhat * second)


def gelu_pair(pre):
    rate = math.sqrt(2.0 / math.pi)
    square = pre * pre
    bend = jnp.tanh(pre * (rate + rate * 0.044715 * square))
    half = 0.5 + 0.5 * bend
    rise = (half - half * half) * (2.0 * rate + 6.0 * rate * 0.044715 * square)
    return pre * half, half + pre * rise


SHIFT_ONE, SCALE_ONE, GATE_ONE, SHIFT_TWO, SCALE_TWO, GATE_TWO, SHIFT_THREE, SCALE_THREE = range(8)


def picker(seg, mod, width):
    return lambda piece: mul(seg[...], mod[:, piece * width : (piece + 1) * width], TN)


def crop_sums(seg, sums, first, values):
    width = sums.shape[1] // len(values)

    @pl.when(first)
    def _():
        sums[...] = jnp.zeros_like(sums)

    for i, value in enumerate(values):
        sums[:, i * width : (i + 1) * width] += mul(seg[:8], value.astype(BF16))


def total_up(parts, total, product):
    at = pl.program_id(0)

    @pl.when(at == 0)
    def _():
        total[...] = product()

    @pl.when((at > 0) & (at < parts))
    def _():
        total[...] += product()

    return at - parts


def rows_of(total, block, step):
    return total[pl.ds(pl.multiple_of(block * step, step), step), :]


def mix_body(attended, seg, mod, embedded, w_proj, b_proj, mixed, projected, hidden):
    pick = picker(seg, mod, w_proj.shape[1])
    project = mul(attended[...], w_proj[...], TN) + b_proj[...]
    projected[...] = project.astype(BF16)
    stream = embedded[...] + pick(GATE_ONE) * project
    mixed[...] = stream
    xhat, _ = normalise(stream)
    hidden[...] = (xhat * (1.0 + pick(SCALE_TWO)) + pick(SHIFT_TWO)).astype(BF16)


def widen(hidden, w_up, b_up, steps, first, count, into=()):
    tokens, width = hidden.shape
    columns = w_up.shape[1]
    part = columns // steps

    def cut(rows):
        return pl.BlockSpec((rows, part), lambda i: (0, i + first))

    return pl.pallas_call(
        up_body,
        grid=(count,),
        in_specs=[pl.BlockSpec((tokens, width), lambda i: (0, 0)), cut(width), cut(1)]
        + [pl.BlockSpec(memory_space=pl.ANY)] * len(into),
        out_specs=[cut(tokens)] * 2,
        out_shape=[jax.ShapeDtypeStruct((tokens, columns), BF16)] * 2,
        input_output_aliases={3 + n: n for n in range(len(into))},
        compiler_params=pltpu.CompilerParams(vmem_limit_bytes=VMEM_BYTES),
        cost_estimate=BRIEF,
        name="widen",
    )(hidden, w_up, b_up, *into)


def up_body(hidden, w_up, b_up, *rest):
    act, slope = rest[-2:]
    activated, rise = gelu_pair(mul(hidden[...], w_up[...]) + b_up[...])
    act[...] = activated.astype(BF16)
    slope[...] = rise.astype(BF16)


def turn_body(
    parts,
    act,
    w_down,
    seg,
    mod,
    mixed,
    grad_tokens,
    b_down,
    w_out,
    b_out,
    grad_mixed,
    grad_mlp,
    token_out,
    grad_out,
    sums,
    total,
):
    block = total_up(parts, total, lambda: mul(act[...], w_down[...]))

    @pl.when(block >= 0)
    def _():
        pick = picker(seg, mod, total.shape[1])
        mlp_out = rows_of(total, block, mixed.shape[0]) + b_down[...]
        gate = pick(GATE_TWO)
        xhat, rate = normalise(mixed[...] + gate * mlp_out)
        scale = pick(SCALE_THREE)
        hidden = (xhat * (1.0 + scale) + pick(SHIFT_THREE)).astype(BF16)
        token_out[...] = (mul(w_out[...], hidden, NT) + b_out[...]).astype(BF16)
        grad_hidden = mul(grad_tokens[...], w_out[...], TN)
        grad = normalise_back(grad_hidden, scale, xhat, rate)
        grad_mixed[...] = grad
        grad_low = (grad * gate).astype(BF16)
        grad_mlp[...] = grad_low
        values = [grad * mlp_out, grad_hidden, grad_hidden * xhat, grad_low]
        crop_sums(seg, sums, block == 0, values)

        @pl.when(block == 0)
        def _():
            grad_out[...] = jnp.zeros_like(grad_out)

        grad_out[...] += mul(grad_tokens[...], hidden)


def gelu_back_body(grad_mlp, slope, seg, w_down, grad_pre, sums):
    grad_act = mul(grad_mlp[...], w_down[...], NT)
    grad_low = (slope[...].astype(F32) * grad_act).astype(BF16)
    grad_pre[...] = grad_low
    sums[...] = mul(seg[:8], grad_low)


def mix_back_body(
    parts,
    grad_pre,
    w_up,
    seg,
    mod,
    mixed,
    grad_two,
    projected,
    w_proj,
    grad_mixed,
    grad_proj,
    grad_att,
    sums,
    total,
):
    block = total_up(parts, total, lambda: mul(grad_pre[...], w_up[...], NT))

    @pl.when(block >= 0)
    def _():
        pick = picker(seg, mod, total.shape[1])
        grad_hidden = rows_of(total, block, mixed.shape[0])
        xhat, rate = normalise(mixed[...])
        grad = grad_two[...] + normalise_back(grad_hidden, pick(SCALE_TWO), xhat, rate)
        grad_mixed[...] = grad
        grad_low = (grad * pick(GATE_ONE)).astype(BF16)
        grad_proj[...] = grad_low
        grad_att[...] = mul(w_proj[...], grad_low, NT).astype(BF16)
        values = [grad * projected[...].astype(F32), grad_hidden, grad_hidden * xhat, grad_low]
        crop_sums(seg, sums, block == 0, values)


def open_back_body(
    parts,
    grad_qkv,
    w_qkv,
    seg,
    mod,
    embedded,
    grad_mixed,
    patches,
    w_embed,
    grad_patches,
    grad_embed,
    qkv_sums,
    sums,
    total,
):
    form = (((0,), (1,)), ((), ()))
    block = total_up(parts, total, lambda: mul(grad_qkv[...], w_qkv[...], form))

    @pl.when(block < 0)
    def _():
        lanes = [
            grad_qkv[:, at : at + LANES].astype(F32) for at in range(0, grad_qkv.shape[1], LANES)
        ]
        qkv_sums[...] = sum(lanes)

    @pl.when(block >= 0)
    def _():
        pick = picker(seg, mod, total.shape[1])
        grad_hidden = rows_of(total, block, embedded.shape[0])
        xhat, rate = normalise(embedded[...])
        grad = grad_mixed[...] + normalise_back(grad_hidden, pick(SCALE_ONE), xhat, rate)
        grad_low = grad.astype(BF16)
        grad_patches[...] = mul(w_embed[...], grad_low, NT)
        crop_sums(seg, sums, block == 0, [grad_hidden, grad_hidden * xhat, grad_low])

        @pl.when(block == 0)
        def _():
            grad_embed[...] = jnp.zeros_like(grad_embed)

        grad_embed[...] += mul(patches[...], grad_low)


def staged(name, body, operands, results, flops, parts=0, blocks=0, total=None):
    def spec(shape, kind, axis, is_input):
        count = (parts, blocks)[kind] if kind in (0, 1) else 1
        if count < 2:
            mode = pl.Buffered(1) if is_input else None
            return pl.BlockSpec(shape, lambda i: (0, 0), pipeline_mode=mode)
        block = tuple(n // count if a == axis else n for a, n in enumerate(shape))

        def place(i):
            at = jnp.minimum(i, parts - 1) if kind == 0 else jnp.maximum(i - parts, 0)
            return (at, 0) if axis == 0 else (0, at)

        return pl.BlockSpec(block, place)

    return pl.pallas_call(
        partial(body, parts) if total is not None else body,
        grid=(parts + blocks,),
        in_specs=[spec(v.shape, kind, axis, True) for v, kind, axis in operands],
        out_specs=[spec(shape, kind, axis, False) for shape, _, kind, axis in results],
        out_shape=[jax.ShapeDtypeStruct(shape, dtype) for shape, dtype, _, _ in results],
        scratch_shapes=[] if total is None else [pltpu.VMEM(total, F32)],
        compiler_params=pltpu.CompilerParams(vmem_limit_bytes=VMEM_BYTES),
        cost_estimate=BRIEF,
        name=name,
    )(*[v for v, _, _ in operands])


def rows_back_body(units, core, lhs, rhs, kept, sent):
    rows = lhs.shape[1] // units
    product = mul(lhs[...], rhs[...], TN).astype(BF16)
    for unit in range(units):
        part = product[unit * rows : (unit + 1) * rows]
        spot = unit // 2

        def keep(spot=spot, part=part):
            kept[spot] = part

        def send(spot=spot, part=part):
            sent[spot] = part

        pl.when(core[0] == unit % 2)(keep)
        pl.when(core[0] != unit % 2)(send)


def rows_back(place, lhs, rhs):
    tokens, deep = lhs.shape
    wide = rhs.shape[1]
    rows = deep // (2 * place.chips)
    steps = next(n for n in (4, 2, 1) if place.chips % n == 0 and deep // n % LANES == 0)
    chips = place.chips // steps
    blocks = pl.BlockSpec((chips, rows, wide), lambda i, core: (i, 0, 0))
    return pl.pallas_call(
        partial(rows_back_body, 2 * chips),
        grid_spec=pltpu.PrefetchScalarGridSpec(
            num_scalar_prefetch=1,
            grid=(steps,),
            in_specs=[
                pl.BlockSpec((tokens, deep // steps), lambda i, core: (0, i)),
                pl.BlockSpec((tokens, wide), lambda i, core: (0, 0)),
            ],
            out_specs=[blocks, blocks],
        ),
        out_shape=[jax.ShapeDtypeStruct((place.chips, rows, wide), BF16)] * 2,
        compiler_params=pltpu.CompilerParams(vmem_limit_bytes=VMEM_BYTES),
        cost_estimate=BRIEF,
        name="rows_back",
    )(place.core[None].astype(jnp.int32), lhs, rhs)


def columns_back_body(form, extra, core, lhs, rhs, *rest):
    product = mul(lhs[...], rhs[...], form)
    wide = product.shape[1]
    out = rest[-1]
    if out.shape[1] > wide:
        tail = jnp.zeros((out.shape[0], out.shape[1] - wide), F32)
        if extra:
            tail = rest[0][...]
        out[:, wide:] = tail.astype(BF16)
    if len(rest) > 1 + extra:
        product = product + rest[extra][:, :wide].astype(F32)
    out[:, :wide] = product.astype(BF16)


def columns_back(lhs, rhs, axis, half, add=(), extra=()):
    tokens, deep = lhs.shape
    wide = rhs.shape[axis] // 2
    steps = 3 if deep % (3 * LANES) == 0 else 1
    padded = -(-wide // LANES) * LANES + sum(v.shape[1] for v in extra)
    out = pl.BlockSpec((deep // steps, padded), lambda i, half: (i, 0))
    if axis == 1:
        right = pl.BlockSpec((tokens, wide), lambda i, half: (0, half[0]))
    else:
        right = pl.BlockSpec((wide, tokens), lambda i, half: (half[0], 0))
    return pl.pallas_call(
        partial(columns_back_body, (((0,), (1 - axis,)), ((), ())), len(extra)),
        grid_spec=pltpu.PrefetchScalarGridSpec(
            num_scalar_prefetch=1,
            grid=(steps,),
            in_specs=[pl.BlockSpec((tokens, deep // steps), lambda i, half: (0, i)), right]
            + [
                pl.BlockSpec((deep // steps, v.shape[1]), lambda i, half: (i, 0))
                for v in extra
            ]
            + [pl.BlockSpec((deep // steps, v.shape[1]), lambda i, half: (i, 0)) for v in add],
            out_specs=out,
        ),
        out_shape=jax.ShapeDtypeStruct((deep, padded), BF16),
        compiler_params=pltpu.CompilerParams(vmem_limit_bytes=VMEM_BYTES),
        cost_estimate=BRIEF,
        name="columns_back",
    )(half[None].astype(jnp.int32), lhs, rhs, *extra, *add)


def split_high(value):
    high = lax.reduce_precision(value, exponent_bits=8, mantissa_bits=7)
    return high.astype(BF16), (value - high).astype(BF16)


def block_tokens(grid, rows, cols):
    seqs, channels = grid.shape[0], grid.shape[-1]
    parts = grid.reshape(seqs, rows, PATCH, cols, PATCH, channels).transpose(0, 2, 4, 5, 1, 3)
    return parts.reshape(seqs, PATCH * PATCH * channels, rows * cols)


def unblock_tokens(parts, rows, cols):
    seqs = parts.shape[0]
    channels = parts.shape[1] // (PATCH * PATCH)
    grid = parts.reshape(seqs, PATCH, PATCH, channels, rows, cols).transpose(0, 4, 1, 5, 2, 3)
    return grid.reshape(seqs, rows * PATCH, cols * PATCH, channels)


def per_device(
    latent,
    conditioning,
    segment_ids,
    positions,
    cotangent,
    w_embed,
    b_embed,
    w_mod,
    b_mod,
    w_qkv,
    b_query,
    b_value,
    w_proj,
    b_proj,
    w_up,
    b_up,
    w_down,
    b_down,
    w_final_mod,
    b_final_mod,
    w_out,
    b_out,
):
    place = Place()
    devices = 2 * place.chips
    rows_all, cols_all = place.size[0], place.size[1]
    group = rows_all * cols_all
    seqs_here, grid_side = segment_ids.shape[:2]
    rows_here, cols_here = latent.shape[1] // PATCH, latent.shape[2] // PATCH
    spot = rows_here * cols_here
    tokens = group * spot
    width = w_embed.shape[1]
    hidden = b_up.shape[0] * devices
    crops = conditioning.shape[1]
    unit = width // devices
    me = (place.at[0] * cols_all + place.at[1]) * place.seqs + lax.axis_index(SEQ)
    slot = place.at[0] * cols_all + place.at[1]
    mine = jnp.minimum(slot, seqs_here - 1)
    active = slot < seqs_here
    p_in, p_out = w_embed.shape[0], b_out.shape[0]

    wide = -(-3 * width // (2 * LANES)) * 2 * LANES
    first = Chain(gather_columns(place, jnp.pad(w_qkv, ((0, 0), (0, wide - 3 * width))), False))
    second = jnp.concatenate([w_up, w_proj, jnp.zeros((unit, LANES), BF16)], axis=1)
    second = Chain(gather_columns(place, second))
    cond_f32 = conditioning.astype(F32).reshape(seqs_here * crops, width)
    sigmoid = jax.nn.sigmoid(cond_f32)
    conds = Chain(gather_seqs(place, (cond_f32 * sigmoid).astype(BF16)))

    packed = jnp.concatenate(
        [
            block_tokens(latent, rows_here, cols_here),
            block_tokens(cotangent, rows_here, cols_here),
            positions.reshape(seqs_here, spot, 2).transpose(0, 2, 1).astype(BF16),
        ],
        axis=1,
    )
    packed = jnp.concatenate([packed, *[packed[-1:]] * (group - seqs_here)], axis=0)
    packed = Chain(one_move(packed, lambda value: exchange(value, GROUP)))

    mod_cols, fin_cols = b_mod.shape[0], b_final_mod.shape[0]
    both_cols = mod_cols + fin_cols
    small = [b_query, b_value, b_proj, b_down, b_embed, b_up, w_out.reshape(-1)]
    sizes = [v.shape[0] for v in small]
    lines = -(-sum(sizes) // both_cols)
    small = jnp.pad(jnp.concatenate(small), (0, lines * both_cols - sum(sizes)))
    start = jnp.concatenate(
        [
            jnp.concatenate(
                [
                    w_mod.reshape(unit, devices, mod_cols).transpose(1, 0, 2),
                    w_final_mod.reshape(unit, devices, fin_cols).transpose(1, 0, 2),
                ],
                axis=2,
            ),
            for_all(small.reshape(lines, both_cols), devices),
        ],
        axis=1,
    )

    start = step([first, conds], start)
    start = step([packed], start)
    start = Chain(one_move(start, exchange))
    step([first, second, conds])
    step([start])
    start = step([first, second], start.result)
    mod_share = start[:, :unit].reshape(width, both_cols)
    small = start[:, unit:].reshape(devices, -1)
    parts, at = [], 0
    for size in sizes:
        parts.append(small[:, at : at + size])
        at += size
    query_bias, value_bias, proj_bias, down_bias, embed_bias, up_bias = [
        p.reshape(-1) for p in parts[:6]
    ]
    out_t = parts[6].reshape(width, p_out).T

    mod_bias = jnp.concatenate([b_mod, b_final_mod]).astype(F32)
    cond_all = finish(conds)
    mod_rows = mul(cond_all.reshape(-1, width), mod_share) + mod_bias
    mod_rows = mod_rows.reshape(place.seqs, seqs_here, crops, both_cols)
    mod_rows = jnp.concatenate([mod_rows, *[mod_rows[:, -1:]] * (group - seqs_here)], axis=1)
    mod_rows = mod_rows.transpose(1, 0, 2, 3).reshape(devices, crops, both_cols)
    mod_rows = step([first, second], mod_rows)
    mod_rows = Chain(one_move(mod_rows, exchange))
    packed = packed.result.transpose(1, 0, 2).reshape(-1, tokens)
    patches_t = packed[:p_in]
    grad_tokens_t = jnp.where(active, packed[p_in : p_in + p_out], 0)
    place_row, place_col = packed[p_in + p_out], packed[p_in + p_out + 1]
    seg = lax.dynamic_index_in_dim(segment_ids, mine, 0, keepdims=False)
    seg = seg.reshape(rows_all, rows_here, cols_all, cols_here).transpose(0, 2, 1, 3)
    seg = seg.reshape(tokens)
    seg_hot = seg[None, :] == jnp.arange(8, dtype=jnp.int32)[:, None]
    real_crop = jnp.arange(8)[:, None] < crops
    seg_key = (seg_hot | (jnp.arange(8)[:, None] == 7)).astype(BF16)
    seg_both = jnp.concatenate([seg_key, seg_key], axis=0)
    seg_query = jnp.where(seg_hot | ~real_crop, 0.0, OUTSIDE).astype(BF16)
    mod_rows = finish(mod_rows).transpose(1, 0, 2)
    modulation = jnp.concatenate(
        [
            mod_rows[..., :mod_cols].reshape(crops, -1),
            mod_rows[..., mod_cols:].reshape(crops, -1),
        ],
        axis=1,
    )
    modulation = jnp.pad(modulation, ((0, 8 - crops), (0, 0)))
    modulation = jnp.concatenate(split_high(modulation), axis=0)

    def by_crop(piece):
        return mul(seg_both, modulation[:, piece * width : (piece + 1) * width], TN)

    quarter = width // 4
    frequency = jnp.exp(jnp.arange(quarter, dtype=F32) / quarter * -math.log(10000.0))
    angle = jnp.arange(grid_side, dtype=F32)[:, None] * frequency
    table_high, table_low = split_high(jnp.concatenate([jnp.sin(angle), jnp.cos(angle)], axis=1))
    blank = jnp.zeros_like(table_high)
    steps = jnp.arange(grid_side, dtype=F32).astype(BF16)[:, None]
    row_hot = (place_row[None] == steps).astype(BF16)
    col_hot = (place_col[None] == steps).astype(BF16)
    embed_lhs = jnp.concatenate(
        [patches_t, row_hot, col_hot, row_hot, col_hot, jnp.ones((16, tokens), BF16)], axis=0
    )
    embed_rhs = jnp.concatenate(
        [
            w_embed,
            jnp.concatenate([table_high, blank], axis=1),
            jnp.concatenate([blank, table_high], axis=1),
            jnp.concatenate([table_low, blank], axis=1),
            jnp.concatenate([blank, table_low], axis=1),
            embed_bias[None],
            jnp.zeros((15, width), BF16),
        ],
        axis=0,
    )
    embedded = mul(embed_lhs, embed_rhs, TN)

    w_down, embedded = step([first, second], w_down, embedded)
    third = Chain(gather_chips(place, w_down, lower_half(width)))
    (qkv_full,) = lay(
        place,
        finish(first),
        [
            [(0, 0, 0, wide // 2, None)],
            [(0, 0, wide // 2, 3 * width - wide // 2, None)],
        ],
        [(place.chips, 2 * unit, 3 * width)],
    )
    qkv_full = qkv_full.reshape(width, 3 * width)
    xhat_one, _ = normalise(embedded)
    hidden_one = (xhat_one * (1.0 + by_crop(SCALE_ONE)) + by_crop(SHIFT_ONE)).astype(BF16)
    qkv_bias = jnp.concatenate([query_bias, jnp.zeros_like(query_bias), value_bias]).astype(F32)
    qkv = (mul(qkv_full, hidden_one, (((0,), (1,)), ((), ()))) + qkv_bias[:, None]).astype(BF16)
    hdim = width // HEADS
    qkv = step([third], qkv).reshape(3 * HEADS, hdim, tokens)
    score_scale = 1.0 / math.sqrt(hdim)
    split = HEADS // 2
    told = (qkv, seg_query, seg_key, score_scale)
    attended, log_total = step([second, third], *attend(*told, 0, split))
    attended, log_total = attend(*told, split, HEADS - split, (attended, log_total))
    attended, log_total = step([second, third], attended, log_total)
    half = (hidden + width + LANES) // 2
    up_full, proj_full = lay(
        place,
        finish(second),
        [
            [(0, 0, 0, half, None)],
            [(0, 0, half, hidden - half, None), (1, hidden - half, 0, width, None)],
        ],
        [(place.chips, 2 * unit, hidden), (place.chips, 2 * unit, width)],
    )
    up_full, proj_full = up_full.reshape(width, hidden), proj_full.reshape(width, width)
    attended_t = attended.reshape(width, tokens)
    blocks = -(-tokens // 256)
    deep = hidden // width
    big = 2 * tokens * width * hidden
    square = 2 * tokens * width * width
    stream = (tokens, width)
    mixed_one, projected, hidden_two = staged(
        "mix",
        mix_body,
        [
            (attended_t, 1, 1),
            (seg_both, 1, 1),
            (modulation, 2, 0),
            (embedded, 1, 0),
            (proj_full, 2, 0),
            (proj_bias[None], 2, 0),
        ],
        [(stream, F32, 1, 0), (stream, BF16, 1, 0), (stream, BF16, 1, 0)],
        square,
        blocks=blocks,
    )
    hidden_two = step([third], hidden_two)
    steps = hidden // (6 * LANES)
    activated = widen(hidden_two, up_full, up_bias[None], steps, 0, steps // 2)
    activated = step([third], *activated)
    activated, slope = widen(
        hidden_two, up_full, up_bias[None], steps, steps // 2, steps - steps // 2, activated
    )
    (down_full,) = lay(
        place,
        finish(third),
        [[(0, 0, 0, width, h)] for h in (0, 1)],
        [(place.chips, 2, w_down.shape[0], width)],
    )
    down_full = down_full.reshape(hidden, width)

    grad_mixed_two, grad_mlp, token_out_t, grad_w_out, turn_sums = staged(
        "turn",
        turn_body,
        [
            (activated, 0, 1),
            (down_full, 0, 0),
            (seg_both, 1, 1),
            (modulation, 2, 0),
            (mixed_one, 1, 0),
            (grad_tokens_t, 1, 1),
            (down_bias[None], 2, 0),
            (out_t, 2, 0),
            (b_out[:, None], 2, 0),
        ],
        [
            (stream, F32, 1, 0),
            (stream, BF16, 1, 0),
            ((p_out, tokens), BF16, 1, 1),
            ((p_out, width), F32, 2, 0),
            ((8, 4 * width), F32, 2, 0),
        ],
        big,
        parts=deep,
        blocks=blocks,
        total=stream,
    )
    down = Chain(scatter_rows(place, *rows_back(place, activated, grad_mlp)))
    grad_pre, up_sums = staged(
        "gelu_back",
        gelu_back_body,
        [(grad_mlp, 2, 0), (slope, 0, 1), (seg_both, 2, 0), (down_full, 0, 0)],
        [((tokens, hidden), BF16, 0, 1), ((8, hidden), F32, 0, 1)],
        big,
        parts=deep,
    )
    back_pre = step([down], grad_pre)

    given = columns_back(hidden_two, back_pre, 1, 1 - place.core)
    given, grad_pre = step([down], given, back_pre)

    def scatter_up():
        (came,) = yield [(given, place.swap)]
        wide = both.shape[1] // 2
        (more,) = yield [(half_of(both, 1 - place.core, wide, 1), place.swap)]
        more = plus(half_of(both, place.core, wide, 1), more).astype(BF16)
        blocks = columns_back(hidden_two, back_pre, 1, place.core, (came,), (more,))
        return (yield from finish_columns(place, blocks))

    up = Chain(scatter_up())
    grad_mixed_one, grad_proj, grad_attended, mix_sums = staged(
        "mix_back",
        mix_back_body,
        [
            (grad_pre, 0, 1),
            (up_full, 0, 1),
            (seg_both, 1, 1),
            (modulation, 2, 0),
            (mixed_one, 1, 0),
            (grad_mixed_two, 1, 0),
            (projected, 1, 0),
            (proj_full, 2, 0),
        ],
        [
            (stream, F32, 1, 0),
            (stream, BF16, 1, 0),
            ((width, tokens), BF16, 1, 1),
            ((8, 4 * width), F32, 2, 0),
        ],
        big + square,
        parts=deep,
        blocks=blocks,
        total=stream,
    )
    both = jnp.concatenate(
        [mul(attended_t, grad_proj), jnp.pad(grad_w_out.T, ((0, 0), (0, LANES - p_out)))], axis=1
    ).astype(BF16)
    both, grad_attended, mix_sums = step([down, up], both, grad_attended, mix_sums)
    early = jnp.concatenate([mix_sums[:crops, : 3 * width], turn_sums[:crops, : 3 * width]], axis=1)
    early = Chain(one_move(for_all(early.astype(BF16), devices), exchange))
    grad_attended = grad_attended.reshape(HEADS, hdim, tokens)
    grad_attended = step([up], grad_attended)
    saved = (qkv, attended, grad_attended, log_total, seg_query, seg_key, score_scale)
    grad_qkv = attend_back(*saved, 0, split)
    grad_qkv = step([down, up], grad_qkv)
    grad_qkv = attend_back(*saved, split, HEADS - split, grad_qkv)
    grad_qkv_t = grad_qkv.reshape(3 * width, tokens)
    given_qkv = columns_back(hidden_one, grad_qkv_t, 0, 1 - place.core)
    given_qkv, grad_qkv_t = step([down, up, early], given_qkv, grad_qkv_t)

    def scatter_qkv():
        came = yield [(given_qkv, place.swap)]
        blocks = columns_back(hidden_one, grad_qkv_t, 0, place.core, came)
        return (yield from finish_columns(place, blocks))

    into_qkv = Chain(scatter_qkv())
    grad_qkv = step([into_qkv], grad_qkv_t)
    grad_patches_t, grad_w_embed, grad_qkv_sum, open_sums = staged(
        "open_back",
        open_back_body,
        [
            (grad_qkv, 0, 0),
            (qkv_full, 0, 1),
            (seg_both, 1, 1),
            (modulation, 2, 0),
            (embedded, 1, 0),
            (grad_mixed_one, 1, 0),
            (patches_t, 1, 1),
            (w_embed, 2, 0),
        ],
        [
            ((p_in, tokens), F32, 1, 1),
            ((p_in, width), F32, 2, 0),
            ((3 * width, LANES), F32, 0, 0),
            ((8, 3 * width), F32, 2, 0),
        ],
        3 * square,
        parts=3,
        blocks=blocks,
        total=stream,
    )
    back = jnp.concatenate([token_out_t.astype(F32), grad_patches_t], axis=0)
    back = back.reshape(-1, group, spot).transpose(1, 0, 2)
    back = Chain(one_move(back, lambda value: exchange(value, GROUP)))
    open_sums, grad_w_embed, grad_qkv_sum = step(
        [into_qkv, up], open_sums, grad_w_embed, grad_qkv_sum
    )

    grad_qkv_sum = jnp.sum(grad_qkv_sum, axis=1)
    sums = [
        open_sums[7, 2 * width :],
        grad_qkv_sum[:width],
        grad_qkv_sum[2 * width :],
        mix_sums[7, 3 * width :],
        turn_sums[7, 3 * width :],
        up_sums[7],
    ]
    sums = [v.reshape(devices, -1) for v in sums]
    sums.append(grad_w_embed.reshape(p_in, devices, unit).transpose(1, 0, 2).reshape(devices, -1))
    sums.append(for_all(jnp.sum(grad_tokens_t.astype(F32), axis=1), devices))
    sums = jnp.concatenate(sums, axis=1)
    count = sums.shape[1]
    late = for_all(open_sums[:crops, : 2 * width].astype(BF16).reshape(-1), devices)
    sums = step([back], jnp.concatenate([*split_high(sums), late], axis=1))
    ends = Chain(one_move(sums, exchange))

    early = early.result.reshape(devices * crops, -1)
    cond_mine = lax.dynamic_slice_in_dim(cond_all, me * unit, unit, 2)
    cond_mine = cond_mine.reshape(place.seqs, seqs_here, crops, unit)
    cond_mine = jnp.concatenate([cond_mine, *[cond_mine[:, -1:]] * (group - seqs_here)], axis=1)
    cond_mine = cond_mine.transpose(1, 0, 2, 3).reshape(devices * crops, unit)
    part_mod = mul(cond_mine, early, TN)
    early_cond = mul(early[:, : 4 * width], w_mod[:, 2 * width :], NT)
    early_cond = early_cond + mul(early[:, 4 * width :], w_final_mod, NT)
    early_sums = jnp.sum(early.astype(F32), axis=0)

    part_mod, early_cond, early_sums = step([up, into_qkv, ends], part_mod, early_cond, early_sums)
    ends = ends.result
    sums = jnp.sum(plus(ends[:, :count], ends[:, count : 2 * count]), axis=0)
    late = ends[:, 2 * count :].reshape(devices * crops, -1)
    shard_biases = [sums[i * unit : (i + 1) * unit] for i in range(5)]
    shard_biases.append(sums[5 * unit : 5 * unit + b_up.shape[0]])
    small_b_out = sums[-p_out:]
    embed_share = sums[5 * unit + b_up.shape[0] : -p_out]
    grad_cond = mul(late, w_mod[:, : 2 * width], NT) + early_cond
    grad_cond = grad_cond.reshape(group, place.seqs, crops, unit)[:seqs_here].transpose(1, 0, 2, 3)
    grad_cond = for_all(grad_cond, group).reshape(devices, -1)
    last = Chain(
        one_move(jnp.concatenate([grad_cond, for_all(embed_share, devices)], axis=1), exchange)
    )
    shard_mod = jnp.concatenate([mul(cond_mine, late, TN), part_mod[:, : 4 * width]], axis=1)
    shard_final = part_mod[:, 4 * width :]
    mod_sums = jnp.concatenate([jnp.sum(late.astype(F32), axis=0), early_sums])
    bias_mod = lax.dynamic_slice_in_dim(mod_sums, me * mod_cols, mod_cols, 0)
    bias_final = lax.dynamic_slice_in_dim(mod_sums, 6 * width + me * fin_cols, fin_cols, 0)

    back = back.result[:seqs_here]
    prediction = unblock_tokens(back[:, :p_out].astype(BF16), rows_here, cols_here)
    grad_latent = unblock_tokens(back[:, p_out:], rows_here, cols_here)

    shard_mod, shard_final = step([into_qkv, last], shard_mod, shard_final)
    last = last.result
    cut = seqs_here * crops * unit
    grad_cond = last[:, :cut].reshape(devices, seqs_here * crops, unit).transpose(1, 0, 2)
    grad_cond = grad_cond.reshape(seqs_here * crops, width)
    grad_conditioning = grad_cond * (sigmoid * (1.0 + cond_f32 * (1.0 - sigmoid)))
    grad_conditioning = grad_conditioning.reshape(seqs_here, crops, width)
    small_w_embed = last[:, cut:].reshape(devices, p_in, unit).transpose(1, 0, 2)
    small_w_embed = small_w_embed.reshape(p_in, width)
    shard_down, shard_up = finish(down), finish(up)
    half = hidden // 2
    cut = half + (width + LANES) // 2
    shard_both = jnp.concatenate([shard_up[:, half:cut], shard_up[:, cut + half :]], axis=1)
    shard_up = jnp.concatenate([shard_up[:, :half], shard_up[:, cut : cut + half]], axis=1)
    shard_qkv = finish(into_qkv)
    half = shard_qkv.shape[1] // 2
    shard_qkv = jnp.concatenate(
        [shard_qkv[:, : 3 * width // 2], shard_qkv[:, half : half + 3 * width // 2]], axis=1
    )
    shard_proj, shard_out = shard_both[:, :width], shard_both[:, width : width + p_out]
    return (
        prediction,
        grad_latent,
        grad_conditioning,
        small_w_embed,
        shard_biases[0],
        shard_mod,
        bias_mod,
        shard_qkv,
        shard_biases[1],
        shard_biases[2],
        shard_proj,
        shard_biases[3],
        shard_up,
        shard_biases[5],
        shard_down,
        shard_biases[4],
        shard_final,
        bias_final,
        shard_out,
        small_b_out,
    )


def solution(mesh):
    grid, seqs, split, rows = P(SEQ, ROW, COL, None), P(SEQ, None, None), P(ALL), P(ALL, None)
    in_specs = (grid, seqs, seqs, grid, grid, P(), split, rows, split, rows, split, split)
    in_specs += (rows, split, rows, split, rows, split, rows, split, rows, P())
    out_specs = (grid, grid, seqs, P(), split, rows, split, rows, split, split)
    out_specs += (rows, split, rows, split, rows, split, rows, split, rows, P())
    return jax.shard_map(
        per_device, mesh=mesh, in_specs=in_specs, out_specs=out_specs, check_vma=False
    )
```

```python
from functools import partial
import math

import jax
import jax.numpy as jnp
from jax import lax
from jax.experimental import pallas as pl
from jax.experimental.pallas import tpu as pltpu
from jax.sharding import PartitionSpec as P

HEADS = 16
PATCH = 2
LANES = 128
ROW, COL, SEQ = "row", "col", "seq"
ALL = (ROW, COL, SEQ)
GROUP = (ROW, COL)
F32 = jnp.float32
BF16 = jnp.bfloat16
OUTSIDE = -1e30
VMEM_BYTES = 56 << 20
BRIEF = pl.CostEstimate(flops=1, bytes_accessed=1, transcendentals=0)
NN = (((1,), (0,)), ((), ()))
NT = (((1,), (1,)), ((), ()))
TN = (((0,), (0,)), ((), ()))


def mul(left, right, form=NN):
    return lax.dot_general(left, right, form, preferred_element_type=F32)


def attend_body(scale, queries, keys, values, seg_query, seg_key, *rest):
    out, log_total = rest[-2:]
    hdim, tokens = queries.shape[1:]
    rate = scale * math.log2(math.e)
    key_side = jnp.concatenate([keys[0], seg_key[...]], axis=0)
    query_side = jnp.concatenate([queries[0], seg_query[...]], axis=0)
    value_side = jnp.concatenate([values[0], jnp.ones((8, tokens), BF16)], axis=0)
    logits = mul(key_side, query_side, TN)
    highest = jnp.max(logits, axis=0, keepdims=True)
    weights = jnp.exp2((logits - highest) * rate)
    summed = mul(value_side, weights.astype(BF16))
    total = summed[hdim : hdim + 1]
    out[0] = (summed[:hdim] / total).astype(BF16)
    log_total[0] = highest * rate + jnp.log2(total)


def attend(qkv, seg_query, seg_key, scale, first, count, into=()):
    triple, hdim, tokens = qkv.shape
    heads = triple // 3

    def head(offset):
        return pl.BlockSpec((1, hdim, tokens), lambda h: (h + offset + first, 0, 0))

    whole = pl.BlockSpec((8, tokens), lambda h: (0, 0))
    return pl.pallas_call(
        partial(attend_body, scale),
        grid=(count,),
        in_specs=[head(0), head(heads), head(2 * heads), whole, whole]
        + [pl.BlockSpec(memory_space=pl.ANY)] * len(into),
        out_specs=[head(0), pl.BlockSpec((1, 1, tokens), lambda h: (h + first, 0, 0))],
        out_shape=[
            jax.ShapeDtypeStruct((heads, hdim, tokens), BF16),
            jax.ShapeDtypeStruct((heads, 1, tokens), F32),
        ],
        input_output_aliases={5 + n: n for n in range(len(into))},
        compiler_params=pltpu.CompilerParams(vmem_limit_bytes=VMEM_BYTES),
        cost_estimate=BRIEF,
        name="attend",
    )(qkv, qkv, qkv, seg_query, seg_key, *into)


def attend_back_body(
    scale, step, queries, keys, values, out, grad_out, log_total, seg_query, seg_key, *rest
):
    grads = rest[-1]
    hdim, tokens = queries.shape[1:]
    rate = scale * math.log2(math.e)
    query_side = jnp.concatenate([queries[0], seg_query[...]], axis=0)
    grad_t = grad_out[0]
    inner = jnp.sum(grad_t.astype(F32) * out[0].astype(F32), axis=0, keepdims=True)
    total = log_total[0]
    query_rows = queries[0].T
    grad_rows = grad_t.T
    grad_query = jnp.zeros((hdim, tokens), F32)
    for start in range(0, tokens, step):
        part = slice(start, start + step)
        key_part = keys[0, :, part]
        key_side = jnp.concatenate([key_part, seg_key[:, part]], axis=0)
        probability = jnp.exp2(mul(key_side, query_side, TN) * rate - total)
        grad_prob = mul(values[0, :, part], grad_t, TN)
        grad_logits = (probability * (grad_prob - inner)).astype(BF16)
        grads[2, 0, :, part] = mul(probability.astype(BF16), grad_rows).T.astype(BF16)
        grads[1, 0, :, part] = (mul(grad_logits, query_rows) * scale).T.astype(BF16)
        grad_query += mul(key_part, grad_logits)
    grads[0, 0] = (grad_query * scale).astype(BF16)


def attend_back(qkv, out, grad_out, log_total, seg_query, seg_key, scale, first, count, into=None):
    triple, hdim, tokens = qkv.shape
    heads = triple // 3

    def head(offset):
        return pl.BlockSpec((1, hdim, tokens), lambda h: (h + offset + first, 0, 0))

    whole = pl.BlockSpec((8, tokens), lambda h: (0, 0))
    given = [] if into is None else [into]
    return pl.pallas_call(
        partial(attend_back_body, scale, min(tokens, 256)),
        grid=(count,),
        in_specs=[
            head(0),
            head(heads),
            head(2 * heads),
            head(0),
            head(0),
            pl.BlockSpec((1, 1, tokens), lambda h: (h + first, 0, 0)),
            whole,
            whole,
        ]
        + [pl.BlockSpec(memory_space=pl.ANY)] * len(given),
        out_specs=pl.BlockSpec((3, 1, hdim, tokens), lambda h: (0, h + first, 0, 0)),
        out_shape=jax.ShapeDtypeStruct((3, heads, hdim, tokens), BF16),
        input_output_aliases={8: 0} if given else {},
        compiler_params=pltpu.CompilerParams(vmem_limit_bytes=VMEM_BYTES),
        cost_estimate=BRIEF,
        name="attend_back",
    )(qkv, qkv, qkv, out, grad_out, log_total, seg_query, seg_key, *given)


class Place:
    def __init__(self):
        self.seqs = lax.axis_size(SEQ)
        self.size = (lax.axis_size(ROW), lax.axis_size(COL), self.seqs // 2)
        seq_at = lax.axis_index(SEQ)
        self.at = (lax.axis_index(ROW), lax.axis_index(COL), seq_at // 2)
        self.core = seq_at % 2
        self.chips = self.size[0] * self.size[1] * self.size[2]

    def shift(self, value, axis, steps=1):
        if axis == 2:
            return lax.ppermute(
                value, SEQ, [(s, (s + 2 * steps) % self.seqs) for s in range(self.seqs)]
            )
        count = self.size[axis]
        return lax.ppermute(value, ALL[axis], [(i, (i + steps) % count) for i in range(count)])

    def swap(self, value):
        return lax.ppermute(value, SEQ, [(s, s ^ 1) for s in range(self.seqs)])

    def mover(self, axis, steps=1):
        return lambda value: self.shift(value, axis, steps)

    def by_core(self, mine, other, axis):
        low = jnp.concatenate([mine, other], axis=axis)
        high = jnp.concatenate([other, mine], axis=axis)
        return jnp.where(self.core == 0, low, high)


class Chain:
    def __init__(self, stages):
        self.stages = stages
        self.result = None
        self.flying = None
        self.ready = next(stages)
        self.launch([value for value, _ in self.ready])

    def launch(self, values):
        self.flying = [move(value) for value, (_, move) in zip(values, self.ready)]
        self.ready = None

    def land(self, came):
        self.flying = None
        try:
            self.ready = self.stages.send(came)
        except StopIteration as end:
            self.result = end.value


def step(chains, *work):
    chains = [c for c in chains if c.flying is not None]
    came, work = lax.optimization_barrier(([c.flying for c in chains], work))
    for chain, values in zip(chains, came):
        chain.land(values)
    going = [c for c in chains if c.ready is not None]
    values, work = lax.optimization_barrier(
        ([[value for value, _ in c.ready] for c in going], work)
    )
    for chain, sent in zip(going, values):
        chain.launch(sent)
    return work[0] if len(work) == 1 else work


def finish(chain):
    while chain.flying is not None:
        chain.land(chain.flying)
        if chain.ready is not None:
            chain.launch([value for value, _ in chain.ready])
    return chain.result


def one_move(value, move):
    (came,) = yield [(value, move)]
    return came


def gather_seqs(place, value):
    xs, x_at = place.size[2], place.at[2]
    (other,) = yield [(value, place.swap)]
    pair = place.by_core(value[None], other[None], 0)
    came = yield [(pair, place.mover(2, back)) for back in range(1, xs)]
    ring = jnp.stack([*came[::-1], pair] * 2)
    ring = lax.dynamic_slice_in_dim(ring, xs - 1 - x_at, xs, 0)
    return ring.reshape(place.seqs, *value.shape)


def gather_chips(place, unit, low, ring=True):
    rows, cols, xs = place.size
    if ring:
        column = [unit]
        for _ in range(1, rows):
            column += yield [(column[-1], place.mover(0))]
    else:
        column = [unit, *(yield [(unit, place.mover(0, back)) for back in range(1, rows)])]
    pieces = {(0, 0): [(0, jnp.stack(column))]}
    swapped = []

    def swaps():
        return [(v, place.swap) for _, v in list_all()[len(swapped) :]]

    def list_all():
        return [((key, at), value) for key, parts in pieces.items() for at, value in parts]

    by_col, by_x = pieces[0, 0][0][1], pieces[0, 0][0][1]
    for hop in range(1, max(cols, xs)):
        going = []
        if hop < cols:
            going.append((by_col, place.mover(1)))
        if hop < xs:
            going.append((by_x, place.mover(2)))
        came = yield going + swaps()
        swapped += came[len(going) :]
        if hop < cols:
            by_col = came[0]
            pieces[hop, 0] = [(0, by_col)]
        if hop < xs:
            by_x = came[len(going) - 1]
            pieces[0, hop] = [(0, by_x)]

    def columns(key, first):
        parts = pieces[key]
        if len(parts) == 2:
            return parts[0 if first else 1][1]
        return parts[0][1][..., :low] if first else parts[0][1][..., low:]

    for total in range(2, cols + xs - 1):
        todo = [(i, total - i) for i in range(1, cols) if 1 <= total - i < xs]
        going = []
        for i, j in todo:
            going.append((columns((i, j - 1), True), place.mover(2)))
            going.append((columns((i - 1, j), False), place.mover(1)))
        came = yield going + swaps()
        swapped += came[len(going) :]
        for n, key in enumerate(todo):
            pieces[key] = [(0, came[2 * n]), (low, came[2 * n + 1])]
    swapped += yield swaps()
    mine = [(key, at, value) for (key, at), value in list_all()]
    other = [(key, at, value) for (key, at, _), value in zip(mine, swapped)]
    return [(0, *p) for p in mine] + [(1, *p) for p in other]


def lay_body(size, static, targets, where, *refs):
    sources, outs = refs[: len(static)], refs[len(static) :]
    for core in (0, 1):

        def run(core=core):
            for ref, (side, key, at, width) in zip(sources, static):
                spots = [
                    lax.rem(where[axis + 1] + size[axis + 1] - back, size[axis + 1])
                    for axis, back in enumerate(key)
                ]
                chip = spots[0] * size[2] + spots[1]
                for out, start, column, wide, split in targets[core if side == 0 else 1 - core]:
                    low, high = max(at, start), min(at + width, start + wide)
                    if low < high:
                        lead = (0, chip) if split is None else (0, chip, split)
                        spot = pl.ds(column + low - start, high - low)
                        outs[out][(*lead, slice(None), spot)] = ref[0, :, low - at : high - at]

        pl.when(where[3] == core)(run)


def lay(place, pieces, targets, shapes):
    where = jnp.stack([*place.at, place.core]).astype(jnp.int32)
    static = [(side, key, at, value.shape[-1]) for side, key, at, value in pieces]
    operands = [p[3] for p in pieces]
    rows = place.size[0]

    def piece(value):
        return pl.BlockSpec((1, *value.shape[1:]), lambda k, where: (k, 0, 0))

    def target(shape):
        rest = (0,) * (len(shape) - 1)
        return pl.BlockSpec(
            (1, *shape[1:]), lambda k, where: (lax.rem(where[0] + rows - k, rows), *rest)
        )

    shapes = [(rows, s[0] // rows, *s[1:]) for s in shapes]
    return pl.pallas_call(
        partial(lay_body, place.size, static, targets),
        grid_spec=pltpu.PrefetchScalarGridSpec(
            num_scalar_prefetch=1,
            grid=(rows,),
            in_specs=[piece(v) for v in operands],
            out_specs=[target(s) for s in shapes],
        ),
        out_shape=[jax.ShapeDtypeStruct(s, BF16) for s in shapes],
        compiler_params=pltpu.CompilerParams(vmem_limit_bytes=VMEM_BYTES),
        cost_estimate=BRIEF,
        name="lay",
    )(where, *operands)


def half_of(value, half, width, axis):
    return lax.dynamic_slice_in_dim(value, half * width, width, axis)


def lower_half(width):
    return width // (2 * LANES) * LANES


def gather_columns(place, shard, ring=True):
    half = shard.shape[1] // 2
    kept = half_of(shard, place.core, half, 1)
    (given,) = yield [(half_of(shard, 1 - place.core, half, 1), place.swap)]
    return (yield from gather_chips(place, place.by_core(kept, given, 0), lower_half(half), ring))


def block_of(blocks, axis, at):
    return lax.dynamic_index_in_dim(blocks, at, axis, keepdims=False)


def plus(*terms):
    return sum(t.astype(F32) for t in terms)


def scatter_chips(place, blocks):
    rows, cols, xs = place.size
    row_at, col_at, x_at = place.at
    if (cols, xs) == (2, 2):
        low = lower_half(blocks.shape[-1])
        by_col, by_x = block_of(blocks, 1, 1 - col_at), block_of(blocks, 1, col_at)
        far, by_col = block_of(by_col, 1, 1 - x_at), block_of(by_col, 1, x_at)
        own, by_x = block_of(by_x, 1, x_at), block_of(by_x, 1, 1 - x_at)
        far_x, far_col = yield [(far[..., :low], place.mover(2)), (far[..., low:], place.mover(1))]
        by_col = jnp.concatenate(
            [plus(by_col[..., :low], far_x).astype(BF16), by_col[..., low:]], axis=-1
        )
        by_x = jnp.concatenate(
            [by_x[..., :low], plus(by_x[..., low:], far_col).astype(BF16)], axis=-1
        )
        from_col, from_x = yield [(by_col, place.mover(1)), (by_x, place.mover(2))]
        own = plus(own, from_col, from_x).astype(BF16)
    else:
        own = blocks
        for axis, spot, count, at in ((2, 2, xs, x_at), (1, 1, cols, col_at)):
            total = block_of(own, spot, lax.rem(at + count - 1, count))
            for back in range(2, count + 1):
                here = block_of(own, spot, lax.rem(at + 2 * count - back, count))
                (given,) = yield [(total, place.mover(axis))]
                total = plus(given, here).astype(BF16)
            own = total
    given = yield [
        (block_of(own, 0, lax.rem(row_at + back, rows)), place.mover(0, back))
        for back in range(1, rows)
    ]
    return plus(block_of(own, 0, row_at), *given)


def finish_columns(place, blocks):
    total = yield from scatter_chips(place, blocks.reshape(*place.size, -1, blocks.shape[1]))
    rows = total.shape[0] // 2
    mine = half_of(total, place.core, rows, 0)
    (other,) = yield [(half_of(total, 1 - place.core, rows, 0), place.swap)]
    return place.by_core(mine, other, 1)


def scatter_rows(place, kept, sent):
    (sent,) = yield [(sent, place.swap)]
    blocks = plus(kept, sent).astype(BF16)
    return (yield from scatter_chips(place, blocks.reshape(*place.size, *kept.shape[1:])))


def exchange(value, axes=ALL):
    return lax.all_to_all(value, axes, 0, 0, tiled=True)


def for_all(value, devices):
    return jnp.broadcast_to(value[None], (devices, *value.shape))


def normalise(stream):
    average = jnp.mean(stream, axis=-1, keepdims=True)
    centred = stream - average
    rate = lax.rsqrt(jnp.mean(centred * centred, axis=-1, keepdims=True) + 1e-06)
    return centred * rate, rate


def normalise_back(grad, scale, xhat, rate):
    inner = grad * (1.0 + scale)
    first = jnp.mean(inner, axis=-1, keepdims=True)
    second = jnp.mean(inner * xhat, axis=-1, keepdims=True)
    return rate * (inner - first - xhat * second)


def gelu_pair(pre):
    rate = math.sqrt(2.0 / math.pi)
    square = pre * pre
    bend = jnp.tanh(pre * (rate + rate * 0.044715 * square))
    half = 0.5 + 0.5 * bend
    rise = (half - half * half) * (2.0 * rate + 6.0 * rate * 0.044715 * square)
    return pre * half, half + pre * rise


SHIFT_ONE, SCALE_ONE, GATE_ONE, SHIFT_TWO, SCALE_TWO, GATE_TWO, SHIFT_THREE, SCALE_THREE = range(8)


def picker(seg, mod, width):
    return lambda piece: mul(seg[...], mod[:, piece * width : (piece + 1) * width], TN)


def crop_sums(seg, sums, first, values):
    width = sums.shape[1] // len(values)

    @pl.when(first)
    def _():
        sums[...] = jnp.zeros_like(sums)

    for i, value in enumerate(values):
        sums[:, i * width : (i + 1) * width] += mul(seg[:8], value.astype(BF16))


def total_up(parts, total, product):
    at = pl.program_id(0)

    @pl.when(at == 0)
    def _():
        total[...] = product()

    @pl.when((at > 0) & (at < parts))
    def _():
        total[...] += product()

    return at - parts


def rows_of(total, block, step):
    return total[pl.ds(pl.multiple_of(block * step, step), step), :]


def mix_body(attended, seg, mod, embedded, w_proj, b_proj, mixed, projected, hidden):
    pick = picker(seg, mod, w_proj.shape[1])
    project = mul(attended[...], w_proj[...], TN) + b_proj[...]
    projected[...] = project.astype(BF16)
    stream = embedded[...] + pick(GATE_ONE) * project
    mixed[...] = stream
    xhat, _ = normalise(stream)
    hidden[...] = (xhat * (1.0 + pick(SCALE_TWO)) + pick(SHIFT_TWO)).astype(BF16)


def widen(hidden, w_up, b_up, steps, first, count, into=()):
    tokens, width = hidden.shape
    columns = w_up.shape[1]
    part = columns // steps

    def cut(rows):
        return pl.BlockSpec((rows, part), lambda i: (0, i + first))

    return pl.pallas_call(
        up_body,
        grid=(count,),
        in_specs=[pl.BlockSpec((tokens, width), lambda i: (0, 0)), cut(width), cut(1)]
        + [pl.BlockSpec(memory_space=pl.ANY)] * len(into),
        out_specs=[cut(tokens)] * 2,
        out_shape=[jax.ShapeDtypeStruct((tokens, columns), BF16)] * 2,
        input_output_aliases={3 + n: n for n in range(len(into))},
        compiler_params=pltpu.CompilerParams(vmem_limit_bytes=VMEM_BYTES),
        cost_estimate=BRIEF,
        name="widen",
    )(hidden, w_up, b_up, *into)


def up_body(hidden, w_up, b_up, *rest):
    act, slope = rest[-2:]
    activated, rise = gelu_pair(mul(hidden[...], w_up[...]) + b_up[...])
    act[...] = activated.astype(BF16)
    slope[...] = rise.astype(BF16)


def turn_body(
    parts,
    act,
    w_down,
    seg,
    mod,
    mixed,
    grad_tokens,
    b_down,
    w_out,
    b_out,
    grad_mixed,
    grad_mlp,
    token_out,
    grad_out,
    sums,
    total,
):
    block = total_up(parts, total, lambda: mul(act[...], w_down[...]))

    @pl.when(block >= 0)
    def _():
        pick = picker(seg, mod, total.shape[1])
        mlp_out = rows_of(total, block, mixed.shape[0]) + b_down[...]
        gate = pick(GATE_TWO)
        xhat, rate = normalise(mixed[...] + gate * mlp_out)
        scale = pick(SCALE_THREE)
        hidden = (xhat * (1.0 + scale) + pick(SHIFT_THREE)).astype(BF16)
        token_out[...] = (mul(w_out[...], hidden, NT) + b_out[...]).astype(BF16)
        grad_hidden = mul(grad_tokens[...], w_out[...], TN)
        grad = normalise_back(grad_hidden, scale, xhat, rate)
        grad_mixed[...] = grad
        grad_low = (grad * gate).astype(BF16)
        grad_mlp[...] = grad_low
        values = [grad * mlp_out, grad_hidden, grad_hidden * xhat, grad_low]
        crop_sums(seg, sums, block == 0, values)

        @pl.when(block == 0)
        def _():
            grad_out[...] = jnp.zeros_like(grad_out)

        grad_out[...] += mul(grad_tokens[...], hidden)


def gelu_back_body(grad_mlp, slope, seg, w_down, grad_pre, sums):
    grad_act = mul(grad_mlp[...], w_down[...], NT)
    grad_low = (slope[...].astype(F32) * grad_act).astype(BF16)
    grad_pre[...] = grad_low
    sums[...] = mul(seg[:8], grad_low)


def mix_back_body(
    parts,
    grad_pre,
    w_up,
    seg,
    mod,
    mixed,
    grad_two,
    projected,
    w_proj,
    grad_mixed,
    grad_proj,
    grad_att,
    sums,
    total,
):
    block = total_up(parts, total, lambda: mul(grad_pre[...], w_up[...], NT))

    @pl.when(block >= 0)
    def _():
        pick = picker(seg, mod, total.shape[1])
        grad_hidden = rows_of(total, block, mixed.shape[0])
        xhat, rate = normalise(mixed[...])
        grad = grad_two[...] + normalise_back(grad_hidden, pick(SCALE_TWO), xhat, rate)
        grad_mixed[...] = grad
        grad_low = (grad * pick(GATE_ONE)).astype(BF16)
        grad_proj[...] = grad_low
        grad_att[...] = mul(w_proj[...], grad_low, NT).astype(BF16)
        values = [grad * projected[...].astype(F32), grad_hidden, grad_hidden * xhat, grad_low]
        crop_sums(seg, sums, block == 0, values)


def open_back_body(
    parts,
    grad_qkv,
    w_qkv,
    seg,
    mod,
    embedded,
    grad_mixed,
    patches,
    w_embed,
    grad_patches,
    grad_embed,
    qkv_sums,
    sums,
    total,
):
    form = (((0,), (1,)), ((), ()))
    block = total_up(parts, total, lambda: mul(grad_qkv[...], w_qkv[...], form))

    @pl.when(block < 0)
    def _():
        lanes = [
            grad_qkv[:, at : at + LANES].astype(F32) for at in range(0, grad_qkv.shape[1], LANES)
        ]
        qkv_sums[...] = sum(lanes)

    @pl.when(block >= 0)
    def _():
        pick = picker(seg, mod, total.shape[1])
        grad_hidden = rows_of(total, block, embedded.shape[0])
        xhat, rate = normalise(embedded[...])
        grad = grad_mixed[...] + normalise_back(grad_hidden, pick(SCALE_ONE), xhat, rate)
        grad_low = grad.astype(BF16)
        grad_patches[...] = mul(w_embed[...], grad_low, NT)
        crop_sums(seg, sums, block == 0, [grad_hidden, grad_hidden * xhat, grad_low])

        @pl.when(block == 0)
        def _():
            grad_embed[...] = jnp.zeros_like(grad_embed)

        grad_embed[...] += mul(patches[...], grad_low)


def staged(name, body, operands, results, flops, parts=0, blocks=0, total=None):
    def spec(shape, kind, axis, is_input):
        count = (parts, blocks)[kind] if kind in (0, 1) else 1
        if count < 2:
            mode = pl.Buffered(1) if is_input else None
            return pl.BlockSpec(shape, lambda i: (0, 0), pipeline_mode=mode)
        block = tuple(n // count if a == axis else n for a, n in enumerate(shape))

        def place(i):
            at = jnp.minimum(i, parts - 1) if kind == 0 else jnp.maximum(i - parts, 0)
            return (at, 0) if axis == 0 else (0, at)

        return pl.BlockSpec(block, place)

    return pl.pallas_call(
        partial(body, parts) if total is not None else body,
        grid=(parts + blocks,),
        in_specs=[spec(v.shape, kind, axis, True) for v, kind, axis in operands],
        out_specs=[spec(shape, kind, axis, False) for shape, _, kind, axis in results],
        out_shape=[jax.ShapeDtypeStruct(shape, dtype) for shape, dtype, _, _ in results],
        scratch_shapes=[] if total is None else [pltpu.VMEM(total, F32)],
        compiler_params=pltpu.CompilerParams(vmem_limit_bytes=VMEM_BYTES),
        cost_estimate=BRIEF,
        name=name,
    )(*[v for v, _, _ in operands])


def rows_back_body(units, core, lhs, rhs, kept, sent):
    rows = lhs.shape[1] // units
    product = mul(lhs[...], rhs[...], TN).astype(BF16)
    for unit in range(units):
        part = product[unit * rows : (unit + 1) * rows]
        spot = unit // 2

        def keep(spot=spot, part=part):
            kept[spot] = part

        def send(spot=spot, part=part):
            sent[spot] = part

        pl.when(core[0] == unit % 2)(keep)
        pl.when(core[0] != unit % 2)(send)


def rows_back(place, lhs, rhs):
    tokens, deep = lhs.shape
    wide = rhs.shape[1]
    rows = deep // (2 * place.chips)
    steps = next(n for n in (4, 2, 1) if place.chips % n == 0 and deep // n % LANES == 0)
    chips = place.chips // steps
    blocks = pl.BlockSpec((chips, rows, wide), lambda i, core: (i, 0, 0))
    return pl.pallas_call(
        partial(rows_back_body, 2 * chips),
        grid_spec=pltpu.PrefetchScalarGridSpec(
            num_scalar_prefetch=1,
            grid=(steps,),
            in_specs=[
                pl.BlockSpec((tokens, deep // steps), lambda i, core: (0, i)),
                pl.BlockSpec((tokens, wide), lambda i, core: (0, 0)),
            ],
            out_specs=[blocks, blocks],
        ),
        out_shape=[jax.ShapeDtypeStruct((place.chips, rows, wide), BF16)] * 2,
        compiler_params=pltpu.CompilerParams(vmem_limit_bytes=VMEM_BYTES),
        cost_estimate=BRIEF,
        name="rows_back",
    )(place.core[None].astype(jnp.int32), lhs, rhs)


def columns_back_body(form, core, lhs, rhs, *rest):
    product = mul(lhs[...], rhs[...], form)
    wide = product.shape[1]
    out = rest[-1]
    if out.shape[1] > wide:
        out[:, wide:] = jnp.zeros((out.shape[0], out.shape[1] - wide), BF16)
    if len(rest) > 1:
        product = product + rest[0][:, :wide].astype(F32)
    out[:, :wide] = product.astype(BF16)


def columns_back(lhs, rhs, axis, half, add=()):
    tokens, deep = lhs.shape
    wide = rhs.shape[axis] // 2
    steps = 3 if deep % (3 * LANES) == 0 else 1
    padded = -(-wide // LANES) * LANES
    out = pl.BlockSpec((deep // steps, padded), lambda i, half: (i, 0))
    if axis == 1:
        right = pl.BlockSpec((tokens, wide), lambda i, half: (0, half[0]))
    else:
        right = pl.BlockSpec((wide, tokens), lambda i, half: (half[0], 0))
    return pl.pallas_call(
        partial(columns_back_body, (((0,), (1 - axis,)), ((), ()))),
        grid_spec=pltpu.PrefetchScalarGridSpec(
            num_scalar_prefetch=1,
            grid=(steps,),
            in_specs=[pl.BlockSpec((tokens, deep // steps), lambda i, half: (0, i)), right]
            + [out] * len(add),
            out_specs=out,
        ),
        out_shape=jax.ShapeDtypeStruct((deep, padded), BF16),
        compiler_params=pltpu.CompilerParams(vmem_limit_bytes=VMEM_BYTES),
        cost_estimate=BRIEF,
        name="columns_back",
    )(half[None].astype(jnp.int32), lhs, rhs, *add)


def split_high(value):
    high = lax.reduce_precision(value, exponent_bits=8, mantissa_bits=7)
    return high.astype(BF16), (value - high).astype(BF16)


def block_tokens(grid, rows, cols):
    seqs, channels = grid.shape[0], grid.shape[-1]
    parts = grid.reshape(seqs, rows, PATCH, cols, PATCH, channels).transpose(0, 2, 4, 5, 1, 3)
    return parts.reshape(seqs, PATCH * PATCH * channels, rows * cols)


def unblock_tokens(parts, rows, cols):
    seqs = parts.shape[0]
    channels = parts.shape[1] // (PATCH * PATCH)
    grid = parts.reshape(seqs, PATCH, PATCH, channels, rows, cols).transpose(0, 4, 1, 5, 2, 3)
    return grid.reshape(seqs, rows * PATCH, cols * PATCH, channels)


def per_device(
    latent,
    conditioning,
    segment_ids,
    positions,
    cotangent,
    w_embed,
    b_embed,
    w_mod,
    b_mod,
    w_qkv,
    b_query,
    b_value,
    w_proj,
    b_proj,
    w_up,
    b_up,
    w_down,
    b_down,
    w_final_mod,
    b_final_mod,
    w_out,
    b_out,
):
    place = Place()
    devices = 2 * place.chips
    rows_all, cols_all = place.size[0], place.size[1]
    group = rows_all * cols_all
    seqs_here, grid_side = segment_ids.shape[:2]
    rows_here, cols_here = latent.shape[1] // PATCH, latent.shape[2] // PATCH
    spot = rows_here * cols_here
    tokens = group * spot
    width = w_embed.shape[1]
    hidden = b_up.shape[0] * devices
    crops = conditioning.shape[1]
    unit = width // devices
    me = (place.at[0] * cols_all + place.at[1]) * place.seqs + lax.axis_index(SEQ)
    slot = place.at[0] * cols_all + place.at[1]
    mine = jnp.minimum(slot, seqs_here - 1)
    active = slot < seqs_here
    p_in, p_out = w_embed.shape[0], b_out.shape[0]

    wide = -(-3 * width // (2 * LANES)) * 2 * LANES
    first = Chain(gather_columns(place, jnp.pad(w_qkv, ((0, 0), (0, wide - 3 * width))), False))
    second = jnp.concatenate([w_up, w_proj, jnp.zeros((unit, LANES), BF16)], axis=1)
    second = Chain(gather_columns(place, second))
    cond_f32 = conditioning.astype(F32).reshape(seqs_here * crops, width)
    sigmoid = jax.nn.sigmoid(cond_f32)
    conds = Chain(gather_seqs(place, (cond_f32 * sigmoid).astype(BF16)))

    latent, cotangent, w_mod = step([first, conds], latent, cotangent, w_mod)
    packed = jnp.concatenate(
        [
            block_tokens(latent, rows_here, cols_here),
            block_tokens(cotangent, rows_here, cols_here),
            positions.reshape(seqs_here, spot, 2).transpose(0, 2, 1).astype(BF16),
        ],
        axis=1,
    )
    packed = jnp.concatenate([packed, *[packed[-1:]] * (group - seqs_here)], axis=0)
    packed = Chain(one_move(packed, lambda value: exchange(value, GROUP)))

    mod_cols, fin_cols = b_mod.shape[0], b_final_mod.shape[0]
    both_cols = mod_cols + fin_cols
    small = [b_query, b_value, b_proj, b_down, b_embed, b_up, w_out.reshape(-1)]
    sizes = [v.shape[0] for v in small]
    lines = -(-sum(sizes) // both_cols)
    small = jnp.pad(jnp.concatenate(small), (0, lines * both_cols - sum(sizes)))
    start = jnp.concatenate(
        [
            jnp.concatenate(
                [
                    w_mod.reshape(unit, devices, mod_cols).transpose(1, 0, 2),
                    w_final_mod.reshape(unit, devices, fin_cols).transpose(1, 0, 2),
                ],
                axis=2,
            ),
            for_all(small.reshape(lines, both_cols), devices),
        ],
        axis=1,
    )

    start = step([first, second, conds, packed], start)
    start = Chain(one_move(start, exchange))
    step([first, second])
    step([start])
    start = start.result
    mod_share = start[:, :unit].reshape(width, both_cols)
    small = start[:, unit:].reshape(devices, -1)
    parts, at = [], 0
    for size in sizes:
        parts.append(small[:, at : at + size])
        at += size
    query_bias, value_bias, proj_bias, down_bias, embed_bias, up_bias = [
        p.reshape(-1) for p in parts[:6]
    ]
    out_t = parts[6].reshape(width, p_out).T

    mod_bias = jnp.concatenate([b_mod, b_final_mod]).astype(F32)
    cond_all = finish(conds)
    mod_rows = mul(cond_all.reshape(-1, width), mod_share) + mod_bias
    mod_rows = mod_rows.reshape(place.seqs, seqs_here, crops, both_cols)
    mod_rows = jnp.concatenate([mod_rows, *[mod_rows[:, -1:]] * (group - seqs_here)], axis=1)
    mod_rows = mod_rows.transpose(1, 0, 2, 3).reshape(devices, crops, both_cols)
    mod_rows = step([first, second], mod_rows)
    mod_rows = Chain(one_move(mod_rows, exchange))
    packed = packed.result.transpose(1, 0, 2).reshape(-1, tokens)
    patches_t = packed[:p_in]
    grad_tokens_t = jnp.where(active, packed[p_in : p_in + p_out], 0)
    place_row, place_col = packed[p_in + p_out], packed[p_in + p_out + 1]
    seg = lax.dynamic_index_in_dim(segment_ids, mine, 0, keepdims=False)
    seg = seg.reshape(rows_all, rows_here, cols_all, cols_here).transpose(0, 2, 1, 3)
    seg = seg.reshape(tokens)
    seg_hot = seg[None, :] == jnp.arange(8, dtype=jnp.int32)[:, None]
    real_crop = jnp.arange(8)[:, None] < crops
    seg_key = (seg_hot | (jnp.arange(8)[:, None] == 7)).astype(BF16)
    seg_both = jnp.concatenate([seg_key, seg_key], axis=0)
    seg_query = jnp.where(seg_hot | ~real_crop, 0.0, OUTSIDE).astype(BF16)
    mod_rows = finish(mod_rows).transpose(1, 0, 2)
    modulation = jnp.concatenate(
        [
            mod_rows[..., :mod_cols].reshape(crops, -1),
            mod_rows[..., mod_cols:].reshape(crops, -1),
        ],
        axis=1,
    )
    modulation = jnp.pad(modulation, ((0, 8 - crops), (0, 0)))
    modulation = jnp.concatenate(split_high(modulation), axis=0)

    def by_crop(piece):
        return mul(seg_both, modulation[:, piece * width : (piece + 1) * width], TN)

    quarter = width // 4
    frequency = jnp.exp(jnp.arange(quarter, dtype=F32) / quarter * -math.log(10000.0))
    angle = jnp.arange(grid_side, dtype=F32)[:, None] * frequency
    table_high, table_low = split_high(jnp.concatenate([jnp.sin(angle), jnp.cos(angle)], axis=1))
    blank = jnp.zeros_like(table_high)
    steps = jnp.arange(grid_side, dtype=F32).astype(BF16)[:, None]
    row_hot = (place_row[None] == steps).astype(BF16)
    col_hot = (place_col[None] == steps).astype(BF16)
    embed_lhs = jnp.concatenate(
        [patches_t, row_hot, col_hot, row_hot, col_hot, jnp.ones((16, tokens), BF16)], axis=0
    )
    embed_rhs = jnp.concatenate(
        [
            w_embed,
            jnp.concatenate([table_high, blank], axis=1),
            jnp.concatenate([blank, table_high], axis=1),
            jnp.concatenate([table_low, blank], axis=1),
            jnp.concatenate([blank, table_low], axis=1),
            embed_bias[None],
            jnp.zeros((15, width), BF16),
        ],
        axis=0,
    )
    embedded = mul(embed_lhs, embed_rhs, TN)

    w_down, embedded = step([first, second], w_down, embedded)
    down_full = lax.all_gather(w_down, ALL, axis=0, tiled=True)
    (qkv_full,) = lay(
        place,
        finish(first),
        [
            [(0, 0, 0, wide // 2, None)],
            [(0, 0, wide // 2, 3 * width - wide // 2, None)],
        ],
        [(place.chips, 2 * unit, 3 * width)],
    )
    qkv_full = qkv_full.reshape(width, 3 * width)
    xhat_one, _ = normalise(embedded)
    hidden_one = (xhat_one * (1.0 + by_crop(SCALE_ONE)) + by_crop(SHIFT_ONE)).astype(BF16)
    qkv_bias = jnp.concatenate([query_bias, jnp.zeros_like(query_bias), value_bias]).astype(F32)
    qkv = (mul(qkv_full, hidden_one, (((0,), (1,)), ((), ()))) + qkv_bias[:, None]).astype(BF16)
    hdim = width // HEADS
    qkv = qkv.reshape(3 * HEADS, hdim, tokens)
    score_scale = 1.0 / math.sqrt(hdim)
    split = HEADS // 2
    told = (qkv, seg_query, seg_key, score_scale)
    attended, log_total = step([second], *attend(*told, 0, split))
    attended, log_total = attend(*told, split, HEADS - split, (attended, log_total))
    attended, log_total = step([second], attended, log_total)
    half = (hidden + width + LANES) // 2
    up_full, proj_full = lay(
        place,
        finish(second),
        [
            [(0, 0, 0, half, None)],
            [(0, 0, half, hidden - half, None), (1, hidden - half, 0, width, None)],
        ],
        [(place.chips, 2 * unit, hidden), (place.chips, 2 * unit, width)],
    )
    up_full, proj_full = up_full.reshape(width, hidden), proj_full.reshape(width, width)
    attended_t = attended.reshape(width, tokens)
    blocks = -(-tokens // 256)
    deep = hidden // width
    big = 2 * tokens * width * hidden
    square = 2 * tokens * width * width
    stream = (tokens, width)
    mixed_one, projected, hidden_two = staged(
        "mix",
        mix_body,
        [
            (attended_t, 1, 1),
            (seg_both, 1, 1),
            (modulation, 2, 0),
            (embedded, 1, 0),
            (proj_full, 2, 0),
            (proj_bias[None], 2, 0),
        ],
        [(stream, F32, 1, 0), (stream, BF16, 1, 0), (stream, BF16, 1, 0)],
        square,
        blocks=blocks,
    )
    steps = hidden // (6 * LANES)
    activated = widen(hidden_two, up_full, up_bias[None], steps, 0, steps // 2)
    activated, slope = widen(
        hidden_two, up_full, up_bias[None], steps, steps // 2, steps - steps // 2, activated
    )

    grad_mixed_two, grad_mlp, token_out_t, grad_w_out, turn_sums = staged(
        "turn",
        turn_body,
        [
            (activated, 0, 1),
            (down_full, 0, 0),
            (seg_both, 1, 1),
            (modulation, 2, 0),
            (mixed_one, 1, 0),
            (grad_tokens_t, 1, 1),
            (down_bias[None], 2, 0),
            (out_t, 2, 0),
            (b_out[:, None], 2, 0),
        ],
        [
            (stream, F32, 1, 0),
            (stream, BF16, 1, 0),
            ((p_out, tokens), BF16, 1, 1),
            ((p_out, width), F32, 2, 0),
            ((8, 4 * width), F32, 2, 0),
        ],
        big,
        parts=deep,
        blocks=blocks,
        total=stream,
    )
    down = Chain(scatter_rows(place, *rows_back(place, activated, grad_mlp)))
    grad_pre, up_sums = staged(
        "gelu_back",
        gelu_back_body,
        [(grad_mlp, 2, 0), (slope, 0, 1), (seg_both, 2, 0), (down_full, 0, 0)],
        [((tokens, hidden), BF16, 0, 1), ((8, hidden), F32, 0, 1)],
        big,
        parts=deep,
    )
    back_pre = step([down], grad_pre)

    given = columns_back(hidden_two, back_pre, 1, 1 - place.core)
    given, grad_pre = step([down], given, back_pre)

    def scatter_up():
        came = yield [(given, place.swap)]
        blocks = columns_back(hidden_two, back_pre, 1, place.core, came)
        return (yield from finish_columns(place, blocks))

    up = Chain(scatter_up())
    grad_pre = step([up], grad_pre)
    grad_mixed_one, grad_proj, grad_attended, mix_sums = staged(
        "mix_back",
        mix_back_body,
        [
            (grad_pre, 0, 1),
            (up_full, 0, 1),
            (seg_both, 1, 1),
            (modulation, 2, 0),
            (mixed_one, 1, 0),
            (grad_mixed_two, 1, 0),
            (projected, 1, 0),
            (proj_full, 2, 0),
        ],
        [
            (stream, F32, 1, 0),
            (stream, BF16, 1, 0),
            ((width, tokens), BF16, 1, 1),
            ((8, 4 * width), F32, 2, 0),
        ],
        big + square,
        parts=deep,
        blocks=blocks,
        total=stream,
    )
    grad_proj, grad_attended, mix_sums = step([down, up], grad_proj, grad_attended, mix_sums)
    early = jnp.concatenate([mix_sums[:crops, : 3 * width], turn_sums[:crops, : 3 * width]], axis=1)
    early = Chain(one_move(early.astype(BF16), lambda v: lax.all_gather(v, ALL, axis=0)))
    grad_attended = grad_attended.reshape(HEADS, hdim, tokens)
    both = jnp.concatenate(
        [mul(attended_t, grad_proj), jnp.pad(grad_w_out.T, ((0, 0), (0, LANES - p_out)))], axis=1
    ).astype(BF16)
    lines = -(-unit // 16) * 16
    both = jnp.pad(both.reshape(devices, unit, -1), ((0, 0), (0, lines - unit), (0, 0)))
    both, grad_attended = step([], both, grad_attended)
    out_proj = Chain(one_move(both, lambda v: lax.psum_scatter(v, ALL, scatter_dimension=0)))
    saved = (qkv, attended, grad_attended, log_total, seg_query, seg_key, score_scale)
    grad_qkv = attend_back(*saved, 0, split)
    grad_qkv = step([down, up], grad_qkv)
    grad_qkv = attend_back(*saved, split, HEADS - split, grad_qkv)
    grad_qkv_t = grad_qkv.reshape(3 * width, tokens)
    given_qkv = columns_back(hidden_one, grad_qkv_t, 0, 1 - place.core)
    given_qkv, grad_qkv_t = step([down, up, early], given_qkv, grad_qkv_t)

    def scatter_qkv():
        came = yield [(given_qkv, place.swap)]
        blocks = columns_back(hidden_one, grad_qkv_t, 0, place.core, came)
        return (yield from finish_columns(place, blocks))

    into_qkv = Chain(scatter_qkv())
    grad_qkv = step([into_qkv], grad_qkv_t)
    grad_patches_t, grad_w_embed, grad_qkv_sum, open_sums = staged(
        "open_back",
        open_back_body,
        [
            (grad_qkv, 0, 0),
            (qkv_full, 0, 1),
            (seg_both, 1, 1),
            (modulation, 2, 0),
            (embedded, 1, 0),
            (grad_mixed_one, 1, 0),
            (patches_t, 1, 1),
            (w_embed, 2, 0),
        ],
        [
            ((p_in, tokens), F32, 1, 1),
            ((p_in, width), F32, 2, 0),
            ((3 * width, LANES), F32, 0, 0),
            ((8, 3 * width), F32, 2, 0),
        ],
        3 * square,
        parts=3,
        blocks=blocks,
        total=stream,
    )
    back = jnp.concatenate([token_out_t.astype(F32), grad_patches_t], axis=0)
    back = back.reshape(-1, group, spot).transpose(1, 0, 2)
    back = Chain(one_move(back, lambda value: exchange(value, GROUP)))
    open_sums, grad_w_embed, grad_qkv_sum = step(
        [into_qkv, up], open_sums, grad_w_embed, grad_qkv_sum
    )

    grad_qkv_sum = jnp.sum(grad_qkv_sum, axis=1)
    sums = [
        open_sums[7, 2 * width :],
        grad_qkv_sum[:width],
        grad_qkv_sum[2 * width :],
        mix_sums[7, 3 * width :],
        turn_sums[7, 3 * width :],
        up_sums[7],
    ]
    sums = [v.reshape(devices, -1) for v in sums]
    sums.append(grad_w_embed.reshape(p_in, devices, unit).transpose(1, 0, 2).reshape(devices, -1))
    sums.append(for_all(jnp.sum(grad_tokens_t.astype(F32), axis=1), devices))
    sums = jnp.concatenate(sums, axis=1)
    count = sums.shape[1]
    late = for_all(open_sums[:crops, : 2 * width].astype(BF16).reshape(-1), devices)
    sums = step([back], jnp.concatenate([*split_high(sums), late], axis=1))
    ends = Chain(one_move(sums, exchange))

    early = step([into_qkv], early.result).reshape(devices * crops, -1)
    cond_mine = lax.dynamic_slice_in_dim(cond_all, me * unit, unit, 2)
    cond_mine = cond_mine.reshape(place.seqs, seqs_here, crops, unit)
    cond_mine = jnp.concatenate([cond_mine, *[cond_mine[:, -1:]] * (group - seqs_here)], axis=1)
    cond_mine = cond_mine.transpose(1, 0, 2, 3).reshape(devices * crops, unit)
    part_mod = mul(cond_mine, early, TN)
    early_cond = mul(early[:, : 4 * width], w_mod[:, 2 * width :], NT)
    early_cond = early_cond + mul(early[:, 4 * width :], w_final_mod, NT)
    early_sums = jnp.sum(early.astype(F32), axis=0)

    part_mod, early_cond, early_sums = step([ends], part_mod, early_cond, early_sums)
    ends = ends.result
    sums = jnp.sum(plus(ends[:, :count], ends[:, count : 2 * count]), axis=0)
    late = ends[:, 2 * count :].reshape(devices * crops, -1)
    shard_biases = [sums[i * unit : (i + 1) * unit] for i in range(5)]
    shard_biases.append(sums[5 * unit : 5 * unit + b_up.shape[0]])
    small_b_out = sums[-p_out:]
    embed_share = sums[5 * unit + b_up.shape[0] : -p_out]
    grad_cond = mul(late, w_mod[:, : 2 * width], NT) + early_cond
    grad_cond = grad_cond.reshape(group, place.seqs, crops, unit)[:seqs_here].transpose(1, 0, 2, 3)
    grad_cond = for_all(grad_cond, group).reshape(devices, -1)
    last = Chain(
        one_move(jnp.concatenate([grad_cond, for_all(embed_share, devices)], axis=1), exchange)
    )
    shard_mod = jnp.concatenate([mul(cond_mine, late, TN), part_mod[:, : 4 * width]], axis=1)
    shard_final = part_mod[:, 4 * width :]
    mod_sums = jnp.concatenate([jnp.sum(late.astype(F32), axis=0), early_sums])
    bias_mod = lax.dynamic_slice_in_dim(mod_sums, me * mod_cols, mod_cols, 0)
    bias_final = lax.dynamic_slice_in_dim(mod_sums, 6 * width + me * fin_cols, fin_cols, 0)

    back = back.result[:seqs_here]
    prediction = unblock_tokens(back[:, :p_out].astype(BF16), rows_here, cols_here)
    grad_latent = unblock_tokens(back[:, p_out:], rows_here, cols_here)

    shard_mod, shard_final = step([into_qkv, last, out_proj], shard_mod, shard_final)
    last = last.result
    cut = seqs_here * crops * unit
    grad_cond = last[:, :cut].reshape(devices, seqs_here * crops, unit).transpose(1, 0, 2)
    grad_cond = grad_cond.reshape(seqs_here * crops, width)
    grad_conditioning = grad_cond * (sigmoid * (1.0 + cond_f32 * (1.0 - sigmoid)))
    grad_conditioning = grad_conditioning.reshape(seqs_here, crops, width)
    small_w_embed = last[:, cut:].reshape(devices, p_in, unit).transpose(1, 0, 2)
    small_w_embed = small_w_embed.reshape(p_in, width)
    shard_down, shard_up, shard_both = finish(down), finish(up), finish(out_proj)
    shard_qkv = finish(into_qkv)
    half = shard_qkv.shape[1] // 2
    shard_qkv = jnp.concatenate(
        [shard_qkv[:, : 3 * width // 2], shard_qkv[:, half : half + 3 * width // 2]], axis=1
    )
    shard_both = shard_both[:unit].astype(F32)
    shard_proj, shard_out = shard_both[:, :width], shard_both[:, width : width + p_out]
    return (
        prediction,
        grad_latent,
        grad_conditioning,
        small_w_embed,
        shard_biases[0],
        shard_mod,
        bias_mod,
        shard_qkv,
        shard_biases[1],
        shard_biases[2],
        shard_proj,
        shard_biases[3],
        shard_up,
        shard_biases[5],
        shard_down,
        shard_biases[4],
        shard_final,
        bias_final,
        shard_out,
        small_b_out,
    )


def solution(mesh):
    grid, seqs, split, rows = P(SEQ, ROW, COL, None), P(SEQ, None, None), P(ALL), P(ALL, None)
    in_specs = (grid, seqs, seqs, grid, grid, P(), split, rows, split, rows, split, split)
    in_specs += (rows, split, rows, split, rows, split, rows, split, rows, P())
    out_specs = (grid, grid, seqs, P(), split, rows, split, rows, split, split)
    out_specs += (rows, split, rows, split, rows, split, rows, split, rows, P())
    return jax.shard_map(
        per_device, mesh=mesh, in_specs=in_specs, out_specs=out_specs, check_vma=False
    )
```

```python
from functools import partial
import math

import jax
import jax.numpy as jnp
from jax import lax
from jax.experimental import pallas as pl
from jax.experimental.pallas import tpu as pltpu
from jax.sharding import PartitionSpec as P

HEADS = 16
PATCH = 2
LANES = 128
ROW, COL, SEQ = "row", "col", "seq"
ALL = (ROW, COL, SEQ)
GROUP = (ROW, COL)
F32 = jnp.float32
BF16 = jnp.bfloat16
OUTSIDE = -1e30
VMEM_BYTES = 56 << 20
BRIEF = pl.CostEstimate(flops=1, bytes_accessed=1, transcendentals=0)
NN = (((1,), (0,)), ((), ()))
NT = (((1,), (1,)), ((), ()))
TN = (((0,), (0,)), ((), ()))


def mul(left, right, form=NN):
    return lax.dot_general(left, right, form, preferred_element_type=F32)


def attend_body(scale, queries, keys, values, seg_query, seg_key, *rest):
    out, log_total = rest[-2:]
    hdim, tokens = queries.shape[1:]
    rate = scale * math.log2(math.e)
    key_side = jnp.concatenate([keys[0], seg_key[...]], axis=0)
    query_side = jnp.concatenate([queries[0], seg_query[...]], axis=0)
    value_side = jnp.concatenate([values[0], jnp.ones((8, tokens), BF16)], axis=0)
    logits = mul(key_side, query_side, TN)
    highest = jnp.max(logits, axis=0, keepdims=True)
    weights = jnp.exp2((logits - highest) * rate)
    summed = mul(value_side, weights.astype(BF16))
    total = summed[hdim : hdim + 1]
    out[0] = (summed[:hdim] / total).astype(BF16)
    log_total[0] = highest * rate + jnp.log2(total)


def attend(qkv, seg_query, seg_key, scale, first, count, into=()):
    triple, hdim, tokens = qkv.shape
    heads = triple // 3

    def head(offset):
        return pl.BlockSpec((1, hdim, tokens), lambda h: (h + offset + first, 0, 0))

    whole = pl.BlockSpec((8, tokens), lambda h: (0, 0))
    return pl.pallas_call(
        partial(attend_body, scale),
        grid=(count,),
        in_specs=[head(0), head(heads), head(2 * heads), whole, whole]
        + [pl.BlockSpec(memory_space=pl.ANY)] * len(into),
        out_specs=[head(0), pl.BlockSpec((1, 1, tokens), lambda h: (h + first, 0, 0))],
        out_shape=[
            jax.ShapeDtypeStruct((heads, hdim, tokens), BF16),
            jax.ShapeDtypeStruct((heads, 1, tokens), F32),
        ],
        input_output_aliases={5 + n: n for n in range(len(into))},
        compiler_params=pltpu.CompilerParams(vmem_limit_bytes=VMEM_BYTES),
        cost_estimate=BRIEF,
        name="attend",
    )(qkv, qkv, qkv, seg_query, seg_key, *into)


def attend_back_body(
    scale, step, queries, keys, values, out, grad_out, log_total, seg_query, seg_key, *rest
):
    grads = rest[-1]
    hdim, tokens = queries.shape[1:]
    rate = scale * math.log2(math.e)
    query_side = jnp.concatenate([queries[0], seg_query[...]], axis=0)
    grad_t = grad_out[0]
    inner = jnp.sum(grad_t.astype(F32) * out[0].astype(F32), axis=0, keepdims=True)
    total = log_total[0]
    query_rows = queries[0].T
    grad_rows = grad_t.T
    grad_query = jnp.zeros((hdim, tokens), F32)
    for start in range(0, tokens, step):
        part = slice(start, start + step)
        key_part = keys[0, :, part]
        key_side = jnp.concatenate([key_part, seg_key[:, part]], axis=0)
        probability = jnp.exp2(mul(key_side, query_side, TN) * rate - total)
        grad_prob = mul(values[0, :, part], grad_t, TN)
        grad_logits = (probability * (grad_prob - inner)).astype(BF16)
        grads[2, 0, :, part] = mul(probability.astype(BF16), grad_rows).T.astype(BF16)
        grads[1, 0, :, part] = (mul(grad_logits, query_rows) * scale).T.astype(BF16)
        grad_query += mul(key_part, grad_logits)
    grads[0, 0] = (grad_query * scale).astype(BF16)


def attend_back(qkv, out, grad_out, log_total, seg_query, seg_key, scale, first, count, into=None):
    triple, hdim, tokens = qkv.shape
    heads = triple // 3

    def head(offset):
        return pl.BlockSpec((1, hdim, tokens), lambda h: (h + offset + first, 0, 0))

    whole = pl.BlockSpec((8, tokens), lambda h: (0, 0))
    given = [] if into is None else [into]
    return pl.pallas_call(
        partial(attend_back_body, scale, min(tokens, 256)),
        grid=(count,),
        in_specs=[
            head(0),
            head(heads),
            head(2 * heads),
            head(0),
            head(0),
            pl.BlockSpec((1, 1, tokens), lambda h: (h + first, 0, 0)),
            whole,
            whole,
        ]
        + [pl.BlockSpec(memory_space=pl.ANY)] * len(given),
        out_specs=pl.BlockSpec((3, 1, hdim, tokens), lambda h: (0, h + first, 0, 0)),
        out_shape=jax.ShapeDtypeStruct((3, heads, hdim, tokens), BF16),
        input_output_aliases={8: 0} if given else {},
        compiler_params=pltpu.CompilerParams(vmem_limit_bytes=VMEM_BYTES),
        cost_estimate=BRIEF,
        name="attend_back",
    )(qkv, qkv, qkv, out, grad_out, log_total, seg_query, seg_key, *given)


class Place:
    def __init__(self):
        self.seqs = lax.axis_size(SEQ)
        self.size = (lax.axis_size(ROW), lax.axis_size(COL), self.seqs // 2)
        seq_at = lax.axis_index(SEQ)
        self.at = (lax.axis_index(ROW), lax.axis_index(COL), seq_at // 2)
        self.core = seq_at % 2
        self.chips = self.size[0] * self.size[1] * self.size[2]

    def shift(self, value, axis, steps=1):
        if axis == 2:
            return lax.ppermute(
                value, SEQ, [(s, (s + 2 * steps) % self.seqs) for s in range(self.seqs)]
            )
        count = self.size[axis]
        return lax.ppermute(value, ALL[axis], [(i, (i + steps) % count) for i in range(count)])

    def swap(self, value):
        return lax.ppermute(value, SEQ, [(s, s ^ 1) for s in range(self.seqs)])

    def mover(self, axis, steps=1):
        return lambda value: self.shift(value, axis, steps)

    def by_core(self, mine, other, axis):
        low = jnp.concatenate([mine, other], axis=axis)
        high = jnp.concatenate([other, mine], axis=axis)
        return jnp.where(self.core == 0, low, high)


class Chain:
    def __init__(self, stages):
        self.stages = stages
        self.result = None
        self.flying = None
        self.ready = next(stages)
        self.launch([value for value, _ in self.ready])

    def launch(self, values):
        self.flying = [move(value) for value, (_, move) in zip(values, self.ready)]
        self.ready = None

    def land(self, came):
        self.flying = None
        try:
            self.ready = self.stages.send(came)
        except StopIteration as end:
            self.result = end.value


def step(chains, *work):
    chains = [c for c in chains if c.flying is not None]
    came, work = lax.optimization_barrier(([c.flying for c in chains], work))
    for chain, values in zip(chains, came):
        chain.land(values)
    going = [c for c in chains if c.ready is not None]
    values, work = lax.optimization_barrier(
        ([[value for value, _ in c.ready] for c in going], work)
    )
    for chain, sent in zip(going, values):
        chain.launch(sent)
    return work[0] if len(work) == 1 else work


def finish(chain):
    while chain.flying is not None:
        chain.land(chain.flying)
        if chain.ready is not None:
            chain.launch([value for value, _ in chain.ready])
    return chain.result


def one_move(value, move):
    (came,) = yield [(value, move)]
    return came


def gather_seqs(place, value):
    xs, x_at = place.size[2], place.at[2]
    (other,) = yield [(value, place.swap)]
    pair = place.by_core(value[None], other[None], 0)
    came = yield [(pair, place.mover(2, back)) for back in range(1, xs)]
    ring = jnp.stack([*came[::-1], pair] * 2)
    ring = lax.dynamic_slice_in_dim(ring, xs - 1 - x_at, xs, 0)
    return ring.reshape(place.seqs, *value.shape)


def gather_chips(place, unit, low, ring=True):
    rows, cols, xs = place.size
    if ring:
        column = [unit]
        for _ in range(1, rows):
            column += yield [(column[-1], place.mover(0))]
    else:
        column = [unit, *(yield [(unit, place.mover(0, back)) for back in range(1, rows)])]
    pieces = {(0, 0): [(0, jnp.stack(column))]}
    swapped = []

    def swaps():
        return [(v, place.swap) for _, v in list_all()[len(swapped) :]]

    def list_all():
        return [((key, at), value) for key, parts in pieces.items() for at, value in parts]

    by_col, by_x = pieces[0, 0][0][1], pieces[0, 0][0][1]
    for hop in range(1, max(cols, xs)):
        going = []
        if hop < cols:
            going.append((by_col, place.mover(1)))
        if hop < xs:
            going.append((by_x, place.mover(2)))
        came = yield going + swaps()
        swapped += came[len(going) :]
        if hop < cols:
            by_col = came[0]
            pieces[hop, 0] = [(0, by_col)]
        if hop < xs:
            by_x = came[len(going) - 1]
            pieces[0, hop] = [(0, by_x)]

    def columns(key, first):
        parts = pieces[key]
        if len(parts) == 2:
            return parts[0 if first else 1][1]
        return parts[0][1][..., :low] if first else parts[0][1][..., low:]

    for total in range(2, cols + xs - 1):
        todo = [(i, total - i) for i in range(1, cols) if 1 <= total - i < xs]
        going = []
        for i, j in todo:
            going.append((columns((i, j - 1), True), place.mover(2)))
            going.append((columns((i - 1, j), False), place.mover(1)))
        came = yield going + swaps()
        swapped += came[len(going) :]
        for n, key in enumerate(todo):
            pieces[key] = [(0, came[2 * n]), (low, came[2 * n + 1])]
    swapped += yield swaps()
    mine = [(key, at, value) for (key, at), value in list_all()]
    other = [(key, at, value) for (key, at, _), value in zip(mine, swapped)]
    return [(0, *p) for p in mine] + [(1, *p) for p in other]


def lay_body(size, static, targets, where, *refs):
    sources, outs = refs[: len(static)], refs[len(static) :]
    for core in (0, 1):

        def run(core=core):
            for ref, (side, key, at, width) in zip(sources, static):
                spots = [
                    lax.rem(where[axis + 1] + size[axis + 1] - back, size[axis + 1])
                    for axis, back in enumerate(key)
                ]
                chip = spots[0] * size[2] + spots[1]
                for out, start, column, wide, split in targets[core if side == 0 else 1 - core]:
                    low, high = max(at, start), min(at + width, start + wide)
                    if low < high:
                        lead = (0, chip) if split is None else (0, chip, split)
                        spot = pl.ds(column + low - start, high - low)
                        outs[out][(*lead, slice(None), spot)] = ref[0, :, low - at : high - at]

        pl.when(where[3] == core)(run)


def lay(place, pieces, targets, shapes):
    where = jnp.stack([*place.at, place.core]).astype(jnp.int32)
    static = [(side, key, at, value.shape[-1]) for side, key, at, value in pieces]
    operands = [p[3] for p in pieces]
    rows = place.size[0]

    def piece(value):
        return pl.BlockSpec((1, *value.shape[1:]), lambda k, where: (k, 0, 0))

    def target(shape):
        rest = (0,) * (len(shape) - 1)
        return pl.BlockSpec(
            (1, *shape[1:]), lambda k, where: (lax.rem(where[0] + rows - k, rows), *rest)
        )

    shapes = [(rows, s[0] // rows, *s[1:]) for s in shapes]
    return pl.pallas_call(
        partial(lay_body, place.size, static, targets),
        grid_spec=pltpu.PrefetchScalarGridSpec(
            num_scalar_prefetch=1,
            grid=(rows,),
            in_specs=[piece(v) for v in operands],
            out_specs=[target(s) for s in shapes],
        ),
        out_shape=[jax.ShapeDtypeStruct(s, BF16) for s in shapes],
        compiler_params=pltpu.CompilerParams(vmem_limit_bytes=VMEM_BYTES),
        cost_estimate=BRIEF,
        name="lay",
    )(where, *operands)


def half_of(value, half, width, axis):
    return lax.dynamic_slice_in_dim(value, half * width, width, axis)


def lower_half(width):
    return width // (2 * LANES) * LANES


def gather_columns(place, shard, ring=True):
    half = shard.shape[1] // 2
    kept = half_of(shard, place.core, half, 1)
    (given,) = yield [(half_of(shard, 1 - place.core, half, 1), place.swap)]
    return (yield from gather_chips(place, place.by_core(kept, given, 0), lower_half(half), ring))


def block_of(blocks, axis, at):
    return lax.dynamic_index_in_dim(blocks, at, axis, keepdims=False)


def plus(*terms):
    return sum(t.astype(F32) for t in terms)


def scatter_chips(place, blocks):
    rows, cols, xs = place.size
    row_at, col_at, x_at = place.at
    if (cols, xs) == (2, 2):
        low = lower_half(blocks.shape[-1])
        by_col, by_x = block_of(blocks, 1, 1 - col_at), block_of(blocks, 1, col_at)
        far, by_col = block_of(by_col, 1, 1 - x_at), block_of(by_col, 1, x_at)
        own, by_x = block_of(by_x, 1, x_at), block_of(by_x, 1, 1 - x_at)
        far_x, far_col = yield [(far[..., :low], place.mover(2)), (far[..., low:], place.mover(1))]
        by_col = jnp.concatenate(
            [plus(by_col[..., :low], far_x).astype(BF16), by_col[..., low:]], axis=-1
        )
        by_x = jnp.concatenate(
            [by_x[..., :low], plus(by_x[..., low:], far_col).astype(BF16)], axis=-1
        )
        from_col, from_x = yield [(by_col, place.mover(1)), (by_x, place.mover(2))]
        own = plus(own, from_col, from_x).astype(BF16)
    else:
        own = blocks
        for axis, spot, count, at in ((2, 2, xs, x_at), (1, 1, cols, col_at)):
            total = block_of(own, spot, lax.rem(at + count - 1, count))
            for back in range(2, count + 1):
                here = block_of(own, spot, lax.rem(at + 2 * count - back, count))
                (given,) = yield [(total, place.mover(axis))]
                total = plus(given, here).astype(BF16)
            own = total
    given = yield [
        (block_of(own, 0, lax.rem(row_at + back, rows)), place.mover(0, back))
        for back in range(1, rows)
    ]
    return plus(block_of(own, 0, row_at), *given)


def finish_columns(place, blocks):
    total = yield from scatter_chips(place, blocks.reshape(*place.size, -1, blocks.shape[1]))
    rows = total.shape[0] // 2
    mine = half_of(total, place.core, rows, 0)
    (other,) = yield [(half_of(total, 1 - place.core, rows, 0), place.swap)]
    return place.by_core(mine, other, 1)


def scatter_rows(place, kept, sent):
    (sent,) = yield [(sent, place.swap)]
    blocks = plus(kept, sent).astype(BF16)
    return (yield from scatter_chips(place, blocks.reshape(*place.size, *kept.shape[1:])))


def exchange(value, axes=ALL):
    return lax.all_to_all(value, axes, 0, 0, tiled=True)


def for_all(value, devices):
    return jnp.broadcast_to(value[None], (devices, *value.shape))


def normalise(stream):
    average = jnp.mean(stream, axis=-1, keepdims=True)
    centred = stream - average
    rate = lax.rsqrt(jnp.mean(centred * centred, axis=-1, keepdims=True) + 1e-06)
    return centred * rate, rate


def normalise_back(grad, scale, xhat, rate):
    inner = grad * (1.0 + scale)
    first = jnp.mean(inner, axis=-1, keepdims=True)
    second = jnp.mean(inner * xhat, axis=-1, keepdims=True)
    return rate * (inner - first - xhat * second)


def gelu_pair(pre):
    rate = math.sqrt(2.0 / math.pi)
    square = pre * pre
    bend = jnp.tanh(pre * (rate + rate * 0.044715 * square))
    half = 0.5 + 0.5 * bend
    rise = (half - half * half) * (2.0 * rate + 6.0 * rate * 0.044715 * square)
    return pre * half, half + pre * rise


SHIFT_ONE, SCALE_ONE, GATE_ONE, SHIFT_TWO, SCALE_TWO, GATE_TWO, SHIFT_THREE, SCALE_THREE = range(8)


def picker(seg, mod, width):
    return lambda piece: mul(seg[...], mod[:, piece * width : (piece + 1) * width], TN)


def crop_sums(seg, sums, first, values):
    width = sums.shape[1] // len(values)

    @pl.when(first)
    def _():
        sums[...] = jnp.zeros_like(sums)

    for i, value in enumerate(values):
        sums[:, i * width : (i + 1) * width] += mul(seg[:8], value.astype(BF16))


def total_up(parts, total, product):
    at = pl.program_id(0)

    @pl.when(at == 0)
    def _():
        total[...] = product()

    @pl.when((at > 0) & (at < parts))
    def _():
        total[...] += product()

    return at - parts


def rows_of(total, block, step):
    return total[pl.ds(pl.multiple_of(block * step, step), step), :]


def mix_body(attended, seg, mod, embedded, w_proj, b_proj, mixed, projected, hidden):
    pick = picker(seg, mod, w_proj.shape[1])
    project = mul(attended[...], w_proj[...], TN) + b_proj[...]
    projected[...] = project.astype(BF16)
    stream = embedded[...] + pick(GATE_ONE) * project
    mixed[...] = stream
    xhat, _ = normalise(stream)
    hidden[...] = (xhat * (1.0 + pick(SCALE_TWO)) + pick(SHIFT_TWO)).astype(BF16)


def widen(hidden, w_up, b_up, steps, first, count, into=()):
    tokens, width = hidden.shape
    columns = w_up.shape[1]
    part = columns // steps

    def cut(rows):
        return pl.BlockSpec((rows, part), lambda i: (0, i + first))

    return pl.pallas_call(
        up_body,
        grid=(count,),
        in_specs=[pl.BlockSpec((tokens, width), lambda i: (0, 0)), cut(width), cut(1)]
        + [pl.BlockSpec(memory_space=pl.ANY)] * len(into),
        out_specs=[cut(tokens)] * 2,
        out_shape=[jax.ShapeDtypeStruct((tokens, columns), BF16)] * 2,
        input_output_aliases={3 + n: n for n in range(len(into))},
        compiler_params=pltpu.CompilerParams(vmem_limit_bytes=VMEM_BYTES),
        cost_estimate=BRIEF,
        name="widen",
    )(hidden, w_up, b_up, *into)


def up_body(hidden, w_up, b_up, *rest):
    act, slope = rest[-2:]
    activated, rise = gelu_pair(mul(hidden[...], w_up[...]) + b_up[...])
    act[...] = activated.astype(BF16)
    slope[...] = rise.astype(BF16)


def turn_body(
    parts,
    act,
    w_down,
    seg,
    mod,
    mixed,
    grad_tokens,
    b_down,
    w_out,
    b_out,
    grad_mixed,
    grad_mlp,
    token_out,
    grad_out,
    sums,
    total,
):
    block = total_up(parts, total, lambda: mul(act[...], w_down[...]))

    @pl.when(block >= 0)
    def _():
        pick = picker(seg, mod, total.shape[1])
        mlp_out = rows_of(total, block, mixed.shape[0]) + b_down[...]
        gate = pick(GATE_TWO)
        xhat, rate = normalise(mixed[...] + gate * mlp_out)
        scale = pick(SCALE_THREE)
        hidden = (xhat * (1.0 + scale) + pick(SHIFT_THREE)).astype(BF16)
        token_out[...] = (mul(w_out[...], hidden, NT) + b_out[...]).astype(BF16)
        grad_hidden = mul(grad_tokens[...], w_out[...], TN)
        grad = normalise_back(grad_hidden, scale, xhat, rate)
        grad_mixed[...] = grad
        grad_low = (grad * gate).astype(BF16)
        grad_mlp[...] = grad_low
        values = [grad * mlp_out, grad_hidden, grad_hidden * xhat, grad_low]
        crop_sums(seg, sums, block == 0, values)

        @pl.when(block == 0)
        def _():
            grad_out[...] = jnp.zeros_like(grad_out)

        grad_out[...] += mul(grad_tokens[...], hidden)


def gelu_back_body(grad_mlp, slope, seg, w_down, grad_pre, sums):
    grad_act = mul(grad_mlp[...], w_down[...], NT)
    grad_low = (slope[...].astype(F32) * grad_act).astype(BF16)
    grad_pre[...] = grad_low
    sums[...] = mul(seg[:8], grad_low)


def mix_back_body(
    parts,
    grad_pre,
    w_up,
    seg,
    mod,
    mixed,
    grad_two,
    projected,
    w_proj,
    grad_mixed,
    grad_proj,
    grad_att,
    sums,
    total,
):
    block = total_up(parts, total, lambda: mul(grad_pre[...], w_up[...], NT))

    @pl.when(block >= 0)
    def _():
        pick = picker(seg, mod, total.shape[1])
        grad_hidden = rows_of(total, block, mixed.shape[0])
        xhat, rate = normalise(mixed[...])
        grad = grad_two[...] + normalise_back(grad_hidden, pick(SCALE_TWO), xhat, rate)
        grad_mixed[...] = grad
        grad_low = (grad * pick(GATE_ONE)).astype(BF16)
        grad_proj[...] = grad_low
        grad_att[...] = mul(w_proj[...], grad_low, NT).astype(BF16)
        values = [grad * projected[...].astype(F32), grad_hidden, grad_hidden * xhat, grad_low]
        crop_sums(seg, sums, block == 0, values)


def open_back_body(
    parts,
    grad_qkv,
    w_qkv,
    seg,
    mod,
    embedded,
    grad_mixed,
    patches,
    w_embed,
    grad_patches,
    grad_embed,
    qkv_sums,
    sums,
    total,
):
    form = (((0,), (1,)), ((), ()))
    block = total_up(parts, total, lambda: mul(grad_qkv[...], w_qkv[...], form))

    @pl.when(block < 0)
    def _():
        lanes = [
            grad_qkv[:, at : at + LANES].astype(F32) for at in range(0, grad_qkv.shape[1], LANES)
        ]
        qkv_sums[...] = sum(lanes)

    @pl.when(block >= 0)
    def _():
        pick = picker(seg, mod, total.shape[1])
        grad_hidden = rows_of(total, block, embedded.shape[0])
        xhat, rate = normalise(embedded[...])
        grad = grad_mixed[...] + normalise_back(grad_hidden, pick(SCALE_ONE), xhat, rate)
        grad_low = grad.astype(BF16)
        grad_patches[...] = mul(w_embed[...], grad_low, NT)
        crop_sums(seg, sums, block == 0, [grad_hidden, grad_hidden * xhat, grad_low])

        @pl.when(block == 0)
        def _():
            grad_embed[...] = jnp.zeros_like(grad_embed)

        grad_embed[...] += mul(patches[...], grad_low)


def staged(name, body, operands, results, flops, parts=0, blocks=0, total=None):
    def spec(shape, kind, axis, is_input):
        count = (parts, blocks)[kind] if kind in (0, 1) else 1
        if count < 2:
            mode = pl.Buffered(1) if is_input else None
            return pl.BlockSpec(shape, lambda i: (0, 0), pipeline_mode=mode)
        block = tuple(n // count if a == axis else n for a, n in enumerate(shape))

        def place(i):
            at = jnp.minimum(i, parts - 1) if kind == 0 else jnp.maximum(i - parts, 0)
            return (at, 0) if axis == 0 else (0, at)

        return pl.BlockSpec(block, place)

    return pl.pallas_call(
        partial(body, parts) if total is not None else body,
        grid=(parts + blocks,),
        in_specs=[spec(v.shape, kind, axis, True) for v, kind, axis in operands],
        out_specs=[spec(shape, kind, axis, False) for shape, _, kind, axis in results],
        out_shape=[jax.ShapeDtypeStruct(shape, dtype) for shape, dtype, _, _ in results],
        scratch_shapes=[] if total is None else [pltpu.VMEM(total, F32)],
        compiler_params=pltpu.CompilerParams(vmem_limit_bytes=VMEM_BYTES),
        cost_estimate=BRIEF,
        name=name,
    )(*[v for v, _, _ in operands])


def rows_back_body(units, core, lhs, rhs, kept, sent):
    rows = lhs.shape[1] // units
    product = mul(lhs[...], rhs[...], TN).astype(BF16)
    for unit in range(units):
        part = product[unit * rows : (unit + 1) * rows]
        spot = unit // 2

        def keep(spot=spot, part=part):
            kept[spot] = part

        def send(spot=spot, part=part):
            sent[spot] = part

        pl.when(core[0] == unit % 2)(keep)
        pl.when(core[0] != unit % 2)(send)


def rows_back(place, lhs, rhs):
    tokens, deep = lhs.shape
    wide = rhs.shape[1]
    rows = deep // (2 * place.chips)
    steps = next(n for n in (4, 2, 1) if place.chips % n == 0 and deep // n % LANES == 0)
    chips = place.chips // steps
    blocks = pl.BlockSpec((chips, rows, wide), lambda i, core: (i, 0, 0))
    return pl.pallas_call(
        partial(rows_back_body, 2 * chips),
        grid_spec=pltpu.PrefetchScalarGridSpec(
            num_scalar_prefetch=1,
            grid=(steps,),
            in_specs=[
                pl.BlockSpec((tokens, deep // steps), lambda i, core: (0, i)),
                pl.BlockSpec((tokens, wide), lambda i, core: (0, 0)),
            ],
            out_specs=[blocks, blocks],
        ),
        out_shape=[jax.ShapeDtypeStruct((place.chips, rows, wide), BF16)] * 2,
        compiler_params=pltpu.CompilerParams(vmem_limit_bytes=VMEM_BYTES),
        cost_estimate=BRIEF,
        name="rows_back",
    )(place.core[None].astype(jnp.int32), lhs, rhs)


def columns_back_body(form, core, lhs, rhs, *rest):
    product = mul(lhs[...], rhs[...], form)
    wide = product.shape[1]
    out = rest[-1]
    if out.shape[1] > wide:
        out[:, wide:] = jnp.zeros((out.shape[0], out.shape[1] - wide), BF16)
    if len(rest) > 1:
        product = product + rest[0][:, :wide].astype(F32)
    out[:, :wide] = product.astype(BF16)


def columns_back(lhs, rhs, axis, half, add=()):
    tokens, deep = lhs.shape
    wide = rhs.shape[axis] // 2
    steps = 3 if deep % (3 * LANES) == 0 else 1
    padded = -(-wide // LANES) * LANES
    out = pl.BlockSpec((deep // steps, padded), lambda i, half: (i, 0))
    if axis == 1:
        right = pl.BlockSpec((tokens, wide), lambda i, half: (0, half[0]))
    else:
        right = pl.BlockSpec((wide, tokens), lambda i, half: (half[0], 0))
    return pl.pallas_call(
        partial(columns_back_body, (((0,), (1 - axis,)), ((), ()))),
        grid_spec=pltpu.PrefetchScalarGridSpec(
            num_scalar_prefetch=1,
            grid=(steps,),
            in_specs=[pl.BlockSpec((tokens, deep // steps), lambda i, half: (0, i)), right]
            + [out] * len(add),
            out_specs=out,
        ),
        out_shape=jax.ShapeDtypeStruct((deep, padded), BF16),
        compiler_params=pltpu.CompilerParams(vmem_limit_bytes=VMEM_BYTES),
        cost_estimate=BRIEF,
        name="columns_back",
    )(half[None].astype(jnp.int32), lhs, rhs, *add)


def split_high(value):
    high = lax.reduce_precision(value, exponent_bits=8, mantissa_bits=7)
    return high.astype(BF16), (value - high).astype(BF16)


def block_tokens(grid, rows, cols):
    seqs, channels = grid.shape[0], grid.shape[-1]
    parts = grid.reshape(seqs, rows, PATCH, cols, PATCH, channels).transpose(0, 2, 4, 5, 1, 3)
    return parts.reshape(seqs, PATCH * PATCH * channels, rows * cols)


def unblock_tokens(parts, rows, cols):
    seqs = parts.shape[0]
    channels = parts.shape[1] // (PATCH * PATCH)
    grid = parts.reshape(seqs, PATCH, PATCH, channels, rows, cols).transpose(0, 4, 1, 5, 2, 3)
    return grid.reshape(seqs, rows * PATCH, cols * PATCH, channels)


def per_device(
    latent,
    conditioning,
    segment_ids,
    positions,
    cotangent,
    w_embed,
    b_embed,
    w_mod,
    b_mod,
    w_qkv,
    b_query,
    b_value,
    w_proj,
    b_proj,
    w_up,
    b_up,
    w_down,
    b_down,
    w_final_mod,
    b_final_mod,
    w_out,
    b_out,
):
    place = Place()
    devices = 2 * place.chips
    rows_all, cols_all = place.size[0], place.size[1]
    group = rows_all * cols_all
    seqs_here, grid_side = segment_ids.shape[:2]
    rows_here, cols_here = latent.shape[1] // PATCH, latent.shape[2] // PATCH
    spot = rows_here * cols_here
    tokens = group * spot
    width = w_embed.shape[1]
    hidden = b_up.shape[0] * devices
    crops = conditioning.shape[1]
    unit = width // devices
    me = (place.at[0] * cols_all + place.at[1]) * place.seqs + lax.axis_index(SEQ)
    slot = place.at[0] * cols_all + place.at[1]
    mine = jnp.minimum(slot, seqs_here - 1)
    active = slot < seqs_here
    p_in, p_out = w_embed.shape[0], b_out.shape[0]

    wide = -(-3 * width // (2 * LANES)) * 2 * LANES
    first = Chain(gather_columns(place, jnp.pad(w_qkv, ((0, 0), (0, wide - 3 * width))), False))
    second = jnp.concatenate([w_up, w_proj, jnp.zeros((unit, LANES), BF16)], axis=1)
    second = Chain(gather_columns(place, second))
    cond_f32 = conditioning.astype(F32).reshape(seqs_here * crops, width)
    sigmoid = jax.nn.sigmoid(cond_f32)
    conds = Chain(gather_seqs(place, (cond_f32 * sigmoid).astype(BF16)))

    latent, cotangent, w_mod = step([first, conds], latent, cotangent, w_mod)
    packed = jnp.concatenate(
        [
            block_tokens(latent, rows_here, cols_here),
            block_tokens(cotangent, rows_here, cols_here),
            positions.reshape(seqs_here, spot, 2).transpose(0, 2, 1).astype(BF16),
        ],
        axis=1,
    )
    packed = jnp.concatenate([packed, *[packed[-1:]] * (group - seqs_here)], axis=0)

    mod_cols, fin_cols = b_mod.shape[0], b_final_mod.shape[0]
    both_cols = mod_cols + fin_cols
    small = [b_query, b_value, b_proj, b_down, b_embed, b_up, w_out.reshape(-1)]
    sizes = [v.shape[0] for v in small]
    lines = -(-sum(sizes) // both_cols)
    small = jnp.pad(jnp.concatenate(small), (0, lines * both_cols - sum(sizes)))
    start = jnp.concatenate(
        [
            jnp.concatenate(
                [
                    w_mod.reshape(unit, devices, mod_cols).transpose(1, 0, 2),
                    w_final_mod.reshape(unit, devices, fin_cols).transpose(1, 0, 2),
                ],
                axis=2,
            ),
            for_all(small.reshape(lines, both_cols), devices),
        ],
        axis=1,
    )

    start = Chain(one_move(start, exchange))
    packed = step([first, second, conds], packed)
    packed = step([start], packed)
    packed = Chain(one_move(packed, lambda value: exchange(value, GROUP)))
    start = start.result
    mod_share = start[:, :unit].reshape(width, both_cols)
    small = start[:, unit:].reshape(devices, -1)
    parts, at = [], 0
    for size in sizes:
        parts.append(small[:, at : at + size])
        at += size
    query_bias, value_bias, proj_bias, down_bias, embed_bias, up_bias = [
        p.reshape(-1) for p in parts[:6]
    ]
    out_t = parts[6].reshape(width, p_out).T

    mod_bias = jnp.concatenate([b_mod, b_final_mod]).astype(F32)
    cond_all = finish(conds)
    mod_rows = mul(cond_all.reshape(-1, width), mod_share) + mod_bias
    mod_rows = mod_rows.reshape(place.seqs, seqs_here, crops, both_cols)
    mod_rows = jnp.concatenate([mod_rows, *[mod_rows[:, -1:]] * (group - seqs_here)], axis=1)
    mod_rows = mod_rows.transpose(1, 0, 2, 3).reshape(devices, crops, both_cols)
    mod_rows = step([first, second, packed], mod_rows)
    mod_rows = Chain(one_move(mod_rows, exchange))
    packed = packed.result.transpose(1, 0, 2).reshape(-1, tokens)
    patches_t = packed[:p_in]
    grad_tokens_t = jnp.where(active, packed[p_in : p_in + p_out], 0)
    place_row, place_col = packed[p_in + p_out], packed[p_in + p_out + 1]
    seg = lax.dynamic_index_in_dim(segment_ids, mine, 0, keepdims=False)
    seg = seg.reshape(rows_all, rows_here, cols_all, cols_here).transpose(0, 2, 1, 3)
    seg = seg.reshape(tokens)
    seg_hot = seg[None, :] == jnp.arange(8, dtype=jnp.int32)[:, None]
    real_crop = jnp.arange(8)[:, None] < crops
    seg_key = (seg_hot | (jnp.arange(8)[:, None] == 7)).astype(BF16)
    seg_both = jnp.concatenate([seg_key, seg_key], axis=0)
    seg_query = jnp.where(seg_hot | ~real_crop, 0.0, OUTSIDE).astype(BF16)
    step([first, second, mod_rows])
    mod_rows = mod_rows.result.transpose(1, 0, 2)
    modulation = jnp.concatenate(
        [
            mod_rows[..., :mod_cols].reshape(crops, -1),
            mod_rows[..., mod_cols:].reshape(crops, -1),
        ],
        axis=1,
    )
    modulation = jnp.pad(modulation, ((0, 8 - crops), (0, 0)))
    modulation = jnp.concatenate(split_high(modulation), axis=0)

    def by_crop(piece):
        return mul(seg_both, modulation[:, piece * width : (piece + 1) * width], TN)

    quarter = width // 4
    frequency = jnp.exp(jnp.arange(quarter, dtype=F32) / quarter * -math.log(10000.0))
    angle = jnp.arange(grid_side, dtype=F32)[:, None] * frequency
    table_high, table_low = split_high(jnp.concatenate([jnp.sin(angle), jnp.cos(angle)], axis=1))
    blank = jnp.zeros_like(table_high)
    steps = jnp.arange(grid_side, dtype=F32).astype(BF16)[:, None]
    row_hot = (place_row[None] == steps).astype(BF16)
    col_hot = (place_col[None] == steps).astype(BF16)
    embed_lhs = jnp.concatenate(
        [patches_t, row_hot, col_hot, row_hot, col_hot, jnp.ones((16, tokens), BF16)], axis=0
    )
    embed_rhs = jnp.concatenate(
        [
            w_embed,
            jnp.concatenate([table_high, blank], axis=1),
            jnp.concatenate([blank, table_high], axis=1),
            jnp.concatenate([table_low, blank], axis=1),
            jnp.concatenate([blank, table_low], axis=1),
            embed_bias[None],
            jnp.zeros((15, width), BF16),
        ],
        axis=0,
    )
    embedded = mul(embed_lhs, embed_rhs, TN)

    xhat_one, _ = normalise(embedded)
    hidden_one = (xhat_one * (1.0 + by_crop(SCALE_ONE)) + by_crop(SHIFT_ONE)).astype(BF16)
    w_down, hidden_one = step([first, second], w_down, hidden_one)
    third = Chain(gather_chips(place, w_down, lower_half(width)))
    (qkv_full,) = lay(
        place,
        finish(first),
        [
            [(0, 0, 0, wide // 2, None)],
            [(0, 0, wide // 2, 3 * width - wide // 2, None)],
        ],
        [(place.chips, 2 * unit, 3 * width)],
    )
    qkv_full = qkv_full.reshape(width, 3 * width)
    qkv_bias = jnp.concatenate([query_bias, jnp.zeros_like(query_bias), value_bias]).astype(F32)
    qkv = (mul(qkv_full, hidden_one, (((0,), (1,)), ((), ()))) + qkv_bias[:, None]).astype(BF16)
    hdim = width // HEADS
    qkv = step([third], qkv).reshape(3 * HEADS, hdim, tokens)
    score_scale = 1.0 / math.sqrt(hdim)
    split = HEADS // 2
    told = (qkv, seg_query, seg_key, score_scale)
    attended, log_total = step([second, third], *attend(*told, 0, split))
    attended, log_total = attend(*told, split, HEADS - split, (attended, log_total))
    attended, log_total = step([second, third], attended, log_total)
    half = (hidden + width + LANES) // 2
    up_full, proj_full = lay(
        place,
        finish(second),
        [
            [(0, 0, 0, half, None)],
            [(0, 0, half, hidden - half, None), (1, hidden - half, 0, width, None)],
        ],
        [(place.chips, 2 * unit, hidden), (place.chips, 2 * unit, width)],
    )
    up_full, proj_full = up_full.reshape(width, hidden), proj_full.reshape(width, width)
    attended_t = attended.reshape(width, tokens)
    blocks = -(-tokens // 256)
    deep = hidden // width
    big = 2 * tokens * width * hidden
    square = 2 * tokens * width * width
    stream = (tokens, width)
    mixed_one, projected, hidden_two = staged(
        "mix",
        mix_body,
        [
            (attended_t, 1, 1),
            (seg_both, 1, 1),
            (modulation, 2, 0),
            (embedded, 1, 0),
            (proj_full, 2, 0),
            (proj_bias[None], 2, 0),
        ],
        [(stream, F32, 1, 0), (stream, BF16, 1, 0), (stream, BF16, 1, 0)],
        square,
        blocks=blocks,
    )
    hidden_two = step([third], hidden_two)
    steps = hidden // (6 * LANES)
    activated = widen(hidden_two, up_full, up_bias[None], steps, 0, steps // 2)
    activated = step([third], *activated)
    activated, slope = widen(
        hidden_two, up_full, up_bias[None], steps, steps // 2, steps - steps // 2, activated
    )

    activated, slope = step([third], activated, slope)
    (down_full,) = lay(
        place,
        finish(third),
        [[(0, 0, 0, width, h)] for h in (0, 1)],
        [(place.chips, 2, w_down.shape[0], width)],
    )
    down_full = down_full.reshape(hidden, width)

    grad_mixed_two, grad_mlp, token_out_t, grad_w_out, turn_sums = staged(
        "turn",
        turn_body,
        [
            (activated, 0, 1),
            (down_full, 0, 0),
            (seg_both, 1, 1),
            (modulation, 2, 0),
            (mixed_one, 1, 0),
            (grad_tokens_t, 1, 1),
            (down_bias[None], 2, 0),
            (out_t, 2, 0),
            (b_out[:, None], 2, 0),
        ],
        [
            (stream, F32, 1, 0),
            (stream, BF16, 1, 0),
            ((p_out, tokens), BF16, 1, 1),
            ((p_out, width), F32, 2, 0),
            ((8, 4 * width), F32, 2, 0),
        ],
        big,
        parts=deep,
        blocks=blocks,
        total=stream,
    )
    down = Chain(scatter_rows(place, *rows_back(place, activated, grad_mlp)))
    grad_pre, up_sums = staged(
        "gelu_back",
        gelu_back_body,
        [(grad_mlp, 2, 0), (slope, 0, 1), (seg_both, 2, 0), (down_full, 0, 0)],
        [((tokens, hidden), BF16, 0, 1), ((8, hidden), F32, 0, 1)],
        big,
        parts=deep,
    )
    back_pre = step([down], grad_pre)

    given = columns_back(hidden_two, back_pre, 1, 1 - place.core)
    given, grad_pre = step([down], given, back_pre)

    def scatter_up():
        came = yield [(given, place.swap)]
        blocks = columns_back(hidden_two, back_pre, 1, place.core, came)
        return (yield from finish_columns(place, blocks))

    up = Chain(scatter_up())
    grad_pre = step([up], grad_pre)
    grad_mixed_one, grad_proj, grad_attended, mix_sums = staged(
        "mix_back",
        mix_back_body,
        [
            (grad_pre, 0, 1),
            (up_full, 0, 1),
            (seg_both, 1, 1),
            (modulation, 2, 0),
            (mixed_one, 1, 0),
            (grad_mixed_two, 1, 0),
            (projected, 1, 0),
            (proj_full, 2, 0),
        ],
        [
            (stream, F32, 1, 0),
            (stream, BF16, 1, 0),
            ((width, tokens), BF16, 1, 1),
            ((8, 4 * width), F32, 2, 0),
        ],
        big + square,
        parts=deep,
        blocks=blocks,
        total=stream,
    )
    grad_proj, grad_attended, mix_sums = step([down, up], grad_proj, grad_attended, mix_sums)
    early = jnp.concatenate([mix_sums[:crops, : 3 * width], turn_sums[:crops, : 3 * width]], axis=1)
    early = Chain(one_move(early.astype(BF16), lambda v: lax.all_gather(v, ALL, axis=0)))
    grad_attended = grad_attended.reshape(HEADS, hdim, tokens)
    both = jnp.concatenate(
        [mul(attended_t, grad_proj), jnp.pad(grad_w_out.T, ((0, 0), (0, LANES - p_out)))], axis=1
    ).astype(BF16)
    lines = -(-unit // 16) * 16
    both = jnp.pad(both.reshape(devices, unit, -1), ((0, 0), (0, lines - unit), (0, 0)))
    both, grad_attended = step([], both, grad_attended)
    out_proj = Chain(one_move(both, lambda v: lax.psum_scatter(v, ALL, scatter_dimension=0)))
    saved = (qkv, attended, grad_attended, log_total, seg_query, seg_key, score_scale)
    grad_qkv = attend_back(*saved, 0, split)
    grad_qkv = step([down, up], grad_qkv)
    grad_qkv = attend_back(*saved, split, HEADS - split, grad_qkv)
    grad_qkv_t = grad_qkv.reshape(3 * width, tokens)
    given_qkv = columns_back(hidden_one, grad_qkv_t, 0, 1 - place.core)
    given_qkv, grad_qkv_t = step([down, up, early], given_qkv, grad_qkv_t)

    def scatter_qkv():
        came = yield [(given_qkv, place.swap)]
        blocks = columns_back(hidden_one, grad_qkv_t, 0, place.core, came)
        return (yield from finish_columns(place, blocks))

    into_qkv = Chain(scatter_qkv())
    grad_qkv = step([into_qkv], grad_qkv_t)
    grad_patches_t, grad_w_embed, grad_qkv_sum, open_sums = staged(
        "open_back",
        open_back_body,
        [
            (grad_qkv, 0, 0),
            (qkv_full, 0, 1),
            (seg_both, 1, 1),
            (modulation, 2, 0),
            (embedded, 1, 0),
            (grad_mixed_one, 1, 0),
            (patches_t, 1, 1),
            (w_embed, 2, 0),
        ],
        [
            ((p_in, tokens), F32, 1, 1),
            ((p_in, width), F32, 2, 0),
            ((3 * width, LANES), F32, 0, 0),
            ((8, 3 * width), F32, 2, 0),
        ],
        3 * square,
        parts=3,
        blocks=blocks,
        total=stream,
    )
    back = jnp.concatenate([token_out_t.astype(F32), grad_patches_t], axis=0)
    back = back.reshape(-1, group, spot).transpose(1, 0, 2)
    back = Chain(one_move(back, lambda value: exchange(value, GROUP)))
    open_sums, grad_w_embed, grad_qkv_sum = step(
        [into_qkv, up], open_sums, grad_w_embed, grad_qkv_sum
    )

    grad_qkv_sum = jnp.sum(grad_qkv_sum, axis=1)
    sums = [
        open_sums[7, 2 * width :],
        grad_qkv_sum[:width],
        grad_qkv_sum[2 * width :],
        mix_sums[7, 3 * width :],
        turn_sums[7, 3 * width :],
        up_sums[7],
    ]
    sums = [v.reshape(devices, -1) for v in sums]
    sums.append(grad_w_embed.reshape(p_in, devices, unit).transpose(1, 0, 2).reshape(devices, -1))
    sums.append(for_all(jnp.sum(grad_tokens_t.astype(F32), axis=1), devices))
    sums = jnp.concatenate(sums, axis=1)
    count = sums.shape[1]
    late = for_all(open_sums[:crops, : 2 * width].astype(BF16).reshape(-1), devices)
    sums = step([back], jnp.concatenate([*split_high(sums), late], axis=1))
    ends = Chain(one_move(sums, exchange))

    early = step([into_qkv], early.result).reshape(devices * crops, -1)
    cond_mine = lax.dynamic_slice_in_dim(cond_all, me * unit, unit, 2)
    cond_mine = cond_mine.reshape(place.seqs, seqs_here, crops, unit)
    cond_mine = jnp.concatenate([cond_mine, *[cond_mine[:, -1:]] * (group - seqs_here)], axis=1)
    cond_mine = cond_mine.transpose(1, 0, 2, 3).reshape(devices * crops, unit)
    part_mod = mul(cond_mine, early, TN)
    early_cond = mul(early[:, : 4 * width], w_mod[:, 2 * width :], NT)
    early_cond = early_cond + mul(early[:, 4 * width :], w_final_mod, NT)
    early_sums = jnp.sum(early.astype(F32), axis=0)

    part_mod, early_cond, early_sums = step([ends], part_mod, early_cond, early_sums)
    ends = ends.result
    sums = jnp.sum(plus(ends[:, :count], ends[:, count : 2 * count]), axis=0)
    late = ends[:, 2 * count :].reshape(devices * crops, -1)
    shard_biases = [sums[i * unit : (i + 1) * unit] for i in range(5)]
    shard_biases.append(sums[5 * unit : 5 * unit + b_up.shape[0]])
    small_b_out = sums[-p_out:]
    embed_share = sums[5 * unit + b_up.shape[0] : -p_out]
    grad_cond = mul(late, w_mod[:, : 2 * width], NT) + early_cond
    grad_cond = grad_cond.reshape(group, place.seqs, crops, unit)[:seqs_here].transpose(1, 0, 2, 3)
    grad_cond = for_all(grad_cond, group).reshape(devices, -1)
    last = Chain(
        one_move(jnp.concatenate([grad_cond, for_all(embed_share, devices)], axis=1), exchange)
    )
    shard_mod = jnp.concatenate([mul(cond_mine, late, TN), part_mod[:, : 4 * width]], axis=1)
    shard_final = part_mod[:, 4 * width :]
    mod_sums = jnp.concatenate([jnp.sum(late.astype(F32), axis=0), early_sums])
    bias_mod = lax.dynamic_slice_in_dim(mod_sums, me * mod_cols, mod_cols, 0)
    bias_final = lax.dynamic_slice_in_dim(mod_sums, 6 * width + me * fin_cols, fin_cols, 0)

    back = back.result[:seqs_here]
    prediction = unblock_tokens(back[:, :p_out].astype(BF16), rows_here, cols_here)
    grad_latent = unblock_tokens(back[:, p_out:], rows_here, cols_here)

    shard_mod, shard_final = step([into_qkv, last, out_proj], shard_mod, shard_final)
    last = last.result
    cut = seqs_here * crops * unit
    grad_cond = last[:, :cut].reshape(devices, seqs_here * crops, unit).transpose(1, 0, 2)
    grad_cond = grad_cond.reshape(seqs_here * crops, width)
    grad_conditioning = grad_cond * (sigmoid * (1.0 + cond_f32 * (1.0 - sigmoid)))
    grad_conditioning = grad_conditioning.reshape(seqs_here, crops, width)
    small_w_embed = last[:, cut:].reshape(devices, p_in, unit).transpose(1, 0, 2)
    small_w_embed = small_w_embed.reshape(p_in, width)
    shard_down, shard_up, shard_both = finish(down), finish(up), finish(out_proj)
    shard_qkv = finish(into_qkv)
    half = shard_qkv.shape[1] // 2
    shard_qkv = jnp.concatenate(
        [shard_qkv[:, : 3 * width // 2], shard_qkv[:, half : half + 3 * width // 2]], axis=1
    )
    shard_both = shard_both[:unit].astype(F32)
    shard_proj, shard_out = shard_both[:, :width], shard_both[:, width : width + p_out]
    return (
        prediction,
        grad_latent,
        grad_conditioning,
        small_w_embed,
        shard_biases[0],
        shard_mod,
        bias_mod,
        shard_qkv,
        shard_biases[1],
        shard_biases[2],
        shard_proj,
        shard_biases[3],
        shard_up,
        shard_biases[5],
        shard_down,
        shard_biases[4],
        shard_final,
        bias_final,
        shard_out,
        small_b_out,
    )


def solution(mesh):
    grid, seqs, split, rows = P(SEQ, ROW, COL, None), P(SEQ, None, None), P(ALL), P(ALL, None)
    in_specs = (grid, seqs, seqs, grid, grid, P(), split, rows, split, rows, split, split)
    in_specs += (rows, split, rows, split, rows, split, rows, split, rows, P())
    out_specs = (grid, grid, seqs, P(), split, rows, split, rows, split, split)
    out_specs += (rows, split, rows, split, rows, split, rows, split, rows, P())
    return jax.shard_map(
        per_device, mesh=mesh, in_specs=in_specs, out_specs=out_specs, check_vma=False
    )
```
